128 devices in a mesh: pts: 32 (over x, y, core), code: 4 (over z).
Axes of the slice: x: 4, y: 4, z: 4, core: 2. Of those that a mesh axis runs over, the one named last changes fastest.
Arguments:
- features: bfloat16 [32768, 512], P('pts'), may hold values from -18 to 18
- codebook: bfloat16 [16384, 512], P('code'), may hold values from -0.25 to 0.25
Outputs:
- new_codes: bfloat16 [16384, 512], P('code')
- row_potential: float32 [32768], P('pts')
- column_potential: float32 [16384], P('code')
The draws below stay inside these ranges and needn't reach their ends.
All inputs are finite; a program needn't handle non-finite values.
Results may differ from the reference program's by a relative error of at most 0.0051.
Values may be sent and summed in bfloat16 or wider, within the bound.
No kernel may reach another device: no remote copies, remote signals or barrier semaphores. Data moves between devices by JAX's collectives and lax.ppermute only.
A program may use at most 128 MiB of HBM per device.

```python
import math
import jax
import jax.numpy as jnp
from jax import lax

D = 512
K = 16384
ITERS = 3
NPTS = 32768


def base_normal(key):
    return jax.random.normal(key, (K, D), jnp.float32)


def draw_codebook(key, part):
    shared = base_normal(key)
    key = jax.random.fold_in(key, 11)
    key_scale = jax.random.fold_in(key, 1)
    row_scale = jax.random.uniform(key_scale, (K, 1), jnp.float32, 0.6, 1.6)
    code_rows = jnp.clip(shared * row_scale / D ** 0.5, -0.25, 0.25)
    return code_rows.astype(jnp.bfloat16)


def draw_features(key, part):
    key = jax.random.fold_in(key, 23)
    key_main = jax.random.fold_in(key, 1)
    key_spread = jax.random.fold_in(key, 2)
    rising = 1.0 + 2.0 * jnp.arange(NPTS, dtype=jnp.float32) / (NPTS - 1)
    noise = jax.random.normal(key_main, (NPTS, D), jnp.float32)
    spread = jnp.exp(jax.random.uniform(key_spread, (NPTS, 1), jnp.float32, -0.5, 0.5))
    drawn = jnp.clip(noise * spread * rising[:, None], -12.0, 12.0)
    return drawn.astype(jnp.bfloat16)


def setup_inputs(seed: int = 0) -> dict:
    arg_keys = jax.random.split(jax.random.key(seed), 3)
    features = draw_features(jax.random.fold_in(arg_keys[2], 71), 0)
    codebook = draw_codebook(jax.random.fold_in(arg_keys[2], 71), 0)
    return {"features": features, "codebook": codebook}


def row_lse(shifted):
    peak_val = jnp.max(shifted, axis=1)
    return peak_val + jnp.log(jnp.sum(jnp.exp(shifted - peak_val[:, None]), axis=1))


def column_update(running, shifted):
    old_peak, old_mass = running
    new_peak = jnp.maximum(old_peak, jnp.max(shifted, axis=0))
    new_mass = old_mass * jnp.exp(old_peak - new_peak) + jnp.sum(jnp.exp(shifted - new_peak[None, :]), axis=0)
    return (new_peak, new_mass)


def reference(features, codebook):
    block_size = math.gcd(NPTS, 1024)
    blocks = features.reshape(NPTS // block_size, block_size, D)
    target_mass = math.log(NPTS / K)
    start_state = (jnp.full((K,), -1e30, jnp.float32), jnp.zeros((K,), jnp.float32))

    def block_logits(block_rows):
        return jnp.dot(block_rows, codebook.T, preferred_element_type=jnp.float32)

    def first_pass(running, block_rows):
        return column_update(running, block_logits(block_rows)), None

    state, _ = lax.scan(first_pass, start_state, blocks)
    col_pot = target_mass - (state[0] + jnp.log(state[1]))

    def merged_pass(col_pot):
        def visit(running, block_rows):
            logits = block_logits(block_rows)
            row_pot = -row_lse(logits + col_pot[None, :])
            return column_update(running, logits + row_pot[:, None]), row_pot

        state, _ = lax.scan(visit, start_state, blocks)
        return target_mass - (state[0] + jnp.log(state[1]))

    for iteration in range(ITERS - 1):
        col_pot = merged_pass(col_pot)

    def closing(running, block_rows):
        logits = block_logits(block_rows)
        row_pot = -row_lse(logits + col_pot[None, :])
        plan = jnp.exp(logits + row_pot[:, None] + col_pot[None, :])
        numer = running[0] + jnp.dot(plan.astype(jnp.bfloat16).T, block_rows, preferred_element_type=jnp.float32)
        denom = running[1] + jnp.sum(plan, axis=0)
        return (numer, denom), row_pot

    zero_state = (jnp.zeros((K, D), jnp.float32), jnp.zeros((K,), jnp.float32))
    (numer, denom), row_pots = lax.scan(closing, zero_state, blocks)
    new_codes = (numer / denom[:, None]).astype(jnp.bfloat16)
    return new_codes, row_pots.reshape(NPTS), col_pot
```

```python
import functools
import math

import jax
import jax.numpy as jnp
from jax import lax
from jax.experimental import pallas as pl
from jax.experimental.pallas import tpu as pltpu
from jax.sharding import PartitionSpec as P

BF = jnp.bfloat16
F32 = jnp.float32
VMEM = 48 * 1024 * 1024
NT = (((1,), (1,)), ((), ()))
NN = (((1,), (0,)), ((), ()))


def place(x, y, c):
    return ((x % 4) * 4 + (y % 4)) * 2 + c


def shift(value, move):
    pairs = []
    for x in range(4):
        for y in range(4):
            for c in range(2):
                pairs.append((place(x, y, c), place(*move(x, y, c))))
    return lax.ppermute(value, "pts", pairs)


def along_x(value, d):
    return shift(value, lambda x, y, c: (x + d, y, c))


def along_y(value, d):
    return shift(value, lambda x, y, c: (x, y + d, c))


def other_core(value):
    return shift(value, lambda x, y, c: (x, y, 1 - c))


def first_axis(value, d):
    return shift(value, lambda x, y, c: (x + d * c, y + d * (1 - c), c))


def second_axis(value, d):
    return shift(value, lambda x, y, c: (x + d * (1 - c), y + d * c, c))


def params():
    return pltpu.CompilerParams(vmem_limit_bytes=VMEM)


def lse_of(parts):
    peak = functools.reduce(jnp.maximum, parts)
    return peak + jnp.log(sum(jnp.exp(p - peak) for p in parts))


def split_rows(v):
    n = v.shape[1]
    hi = v.astype(BF).astype(F32)
    mid = (v - hi).astype(BF).astype(F32)
    low = v - hi - mid
    row = lax.broadcasted_iota(jnp.int32, (16, n), 0)
    return jnp.where(row == 0, hi, jnp.where(row == 1, mid, jnp.where(row == 2, low, 0.0))).astype(BF)


def to_row(col):
    n = col.shape[0]
    diag = lax.broadcasted_iota(jnp.int32, (128, 128), 0) == lax.broadcasted_iota(jnp.int32, (128, 128), 1)
    parts = []
    for i in range(0, n, 128):
        parts.append(jnp.sum(jnp.where(diag, col[i : i + 128], 0.0), axis=0, keepdims=True))
    return jnp.concatenate(parts, axis=1)


def columns(core, feats, codebook, codes, bc=256):
    rows = feats.shape[0]

    def kern(core_ref, f_ref, c_ref, o_ref):
        logits = lax.dot_general(f_ref[...], c_ref[...], NT, preferred_element_type=F32)
        peak = jnp.max(logits, axis=0, keepdims=True)
        o_ref[...] = peak + jnp.log(jnp.sum(jnp.exp(logits - peak), axis=0, keepdims=True))

    return pl.pallas_call(
        kern,
        out_shape=jax.ShapeDtypeStruct((1, codes), F32),
        grid_spec=pltpu.PrefetchScalarGridSpec(
            num_scalar_prefetch=1,
            grid=(codes // bc,),
            in_specs=[
                pl.BlockSpec((rows, feats.shape[1]), lambda j, core: (0, 0)),
                pl.BlockSpec((bc, feats.shape[1]), lambda j, core: (core[0] * (codes // bc) + j, 0)),
            ],
            out_specs=pl.BlockSpec((1, bc), lambda j, core: (0, j)),
        ),
        compiler_params=params(),
        name="columns",
    )(core, feats, codebook)


def rows_first(core, feats, codebook, parts, target, codes, rb=256):
    rows, width = feats.shape

    def kern(core_ref, f_ref, c_ref, p0, p1, p2, p3, a_ref, lse_ref, peak_ref, col_ref):
        @pl.when(pl.program_id(0) == 0)
        def _():
            col_ref[...] = target - lse_of([p0[...], p1[...], p2[...], p3[...]])

        for s in range(0, rb, 128):
            val = lax.dot_general(f_ref[pl.ds(s, 128), :], c_ref[...], NT, preferred_element_type=F32) + col_ref[...]
            peak = jnp.max(val, axis=1, keepdims=True)
            ex = jnp.exp(val - peak)
            total = jnp.sum(ex, axis=1, keepdims=True)
            a_ref[pl.ds(s, 128), :] = ex.astype(BF)
            lse_ref[:, :, pl.ds(s, 128)] = jnp.broadcast_to(to_row(peak + jnp.log(total))[None], (8, 1, 128))
            peak_ref[:, pl.ds(s, 128)] = to_row(peak)

    vec = pl.BlockSpec((1, codes), lambda i, core: (0, 0))
    return pl.pallas_call(
        kern,
        out_shape=(
            jax.ShapeDtypeStruct((rows, codes), BF),
            jax.ShapeDtypeStruct((8, 1, rows), F32),
            jax.ShapeDtypeStruct((1, rows), F32),
            jax.ShapeDtypeStruct((1, codes), F32),
        ),
        grid_spec=pltpu.PrefetchScalarGridSpec(
            num_scalar_prefetch=1,
            grid=(rows // rb,),
            in_specs=[
                pl.BlockSpec((rb, width), lambda i, core: (i, 0)),
                pl.BlockSpec((codes, width), lambda i, core: (core[0], 0)),
                vec, vec, vec, vec,
            ],
            out_specs=(
                pl.BlockSpec((rb, codes), lambda i, core: (i, 0)),
                pl.BlockSpec((8, 1, rb), lambda i, core: (0, 0, i)),
                pl.BlockSpec((1, rb), lambda i, core: (0, i)),
                vec,
            ),
        ),
        compiler_params=params(),
        name="rows_first",
    )(core, feats, codebook, *parts)


def col_sums_first(scaled, lses, peak, rb=512):
    rows, codes = scaled.shape

    def kern(a_ref, l_ref, p_ref, s_ref, r_ref, w_ref, lhs):
        i = pl.program_id(0)

        @pl.when(i == 0)
        def _():
            pot = -lse_of([l_ref[k] for k in range(8)])
            weight = jnp.exp(p_ref[...] + pot)
            r_ref[...] = pot
            w_ref[...] = weight
            for b in range(rows // rb):
                lhs[b] = split_rows(weight[:, b * rb : (b + 1) * rb])
            s_ref[...] = jnp.zeros_like(s_ref)

        out = lax.dot_general(lhs[i], a_ref[...], NN, preferred_element_type=F32)
        s_ref[...] += jnp.sum(out, axis=0, keepdims=True)

    return pl.pallas_call(
        kern,
        out_shape=(
            jax.ShapeDtypeStruct((1, codes), F32),
            jax.ShapeDtypeStruct((1, rows), F32),
            jax.ShapeDtypeStruct((1, rows), F32),
        ),
        grid=(rows // rb,),
        in_specs=[
            pl.BlockSpec((rb, codes), lambda i: (i, 0)),
            pl.BlockSpec((8, 1, rows), lambda i: (0, 0, 0)),
            pl.BlockSpec((1, rows), lambda i: (0, 0)),
        ],
        out_specs=(
            pl.BlockSpec((1, codes), lambda i: (0, 0)),
            pl.BlockSpec((1, rows), lambda i: (0, 0)),
            pl.BlockSpec((1, rows), lambda i: (0, 0)),
        ),
        scratch_shapes=[pltpu.VMEM((rows // rb, 16, rb), BF)],
        compiler_params=params(),
        name="col_sums_first",
    )(scaled, lses, peak)


def col_sums(scaled, totals, weight, rb=512):
    rows, codes = scaled.shape

    def kern(a_ref, t_ref, w_ref, s_ref, lhs):
        i = pl.program_id(0)

        @pl.when(i == 0)
        def _():
            rho = w_ref[...] / sum(t_ref[k] for k in range(8))
            for b in range(rows // rb):
                lhs[b] = split_rows(rho[:, b * rb : (b + 1) * rb])
            s_ref[...] = jnp.zeros_like(s_ref)

        out = lax.dot_general(lhs[i], a_ref[...], NN, preferred_element_type=F32)
        s_ref[...] += jnp.sum(out, axis=0, keepdims=True)

    return pl.pallas_call(
        kern,
        out_shape=jax.ShapeDtypeStruct((1, codes), F32),
        grid=(rows // rb,),
        in_specs=[
            pl.BlockSpec((rb, codes), lambda i: (i, 0)),
            pl.BlockSpec((8, 1, rows), lambda i: (0, 0, 0)),
            pl.BlockSpec((1, rows), lambda i: (0, 0)),
        ],
        out_specs=pl.BlockSpec((1, codes), lambda i: (0, 0)),
        scratch_shapes=[pltpu.VMEM((rows // rb, 16, rb), BF)],
        compiler_params=params(),
        name="col_sums",
    )(scaled, totals, weight)


def row_sums(scaled, weight, parts, first_col, scale, rb=512):
    rows, codes = scaled.shape

    def kern(a_ref, w_ref, p0, p1, p2, p3, c_ref, t_ref, col_ref, lhs):
        @pl.when(pl.program_id(0) == 0)
        def _():
            ratio = scale / (p0[...] + p1[...] + p2[...] + p3[...])
            col_ref[...] = c_ref[...] + jnp.log(ratio)
            lhs[...] = split_rows(ratio)

        out = lax.dot_general(lhs[...], a_ref[...], NT, preferred_element_type=F32)
        total = jnp.sum(out, axis=0, keepdims=True) * w_ref[...]
        t_ref[...] = jnp.broadcast_to(total[None], t_ref.shape)

    vec = pl.BlockSpec((1, codes), lambda i: (0, 0))
    return pl.pallas_call(
        kern,
        out_shape=(jax.ShapeDtypeStruct((8, 1, rows), F32), jax.ShapeDtypeStruct((1, codes), F32)),
        grid=(rows // rb,),
        in_specs=[
            pl.BlockSpec((rb, codes), lambda i: (i, 0)),
            pl.BlockSpec((1, rb), lambda i: (0, i)),
            vec, vec, vec, vec, vec,
        ],
        out_specs=(pl.BlockSpec((8, 1, rb), lambda i: (0, 0, i)), vec),
        scratch_shapes=[pltpu.VMEM((16, codes), BF)],
        compiler_params=params(),
        name="row_sums",
    )(scaled, weight, *parts, first_col)


def weigh(feats_t, totals, weight, first_row, lb=512):
    width, rows = feats_t.shape

    def kern(f_ref, t_ref, w_ref, r_ref, lhs_ref, row_ref):
        total = sum(t_ref[k] for k in range(8))
        rho = w_ref[...] / total
        row_ref[...] = r_ref[...] - jnp.log(total)
        lhs_ref[pl.ds(0, width), :] = (f_ref[...].astype(F32) * rho).astype(BF)
        lhs_ref[pl.ds(width, 16), :] = split_rows(rho)

    return pl.pallas_call(
        kern,
        out_shape=(jax.ShapeDtypeStruct((width + 16, rows), BF), jax.ShapeDtypeStruct((1, rows), F32)),
        grid=(rows // lb,),
        in_specs=[
            pl.BlockSpec((width, lb), lambda i: (0, i)),
            pl.BlockSpec((8, 1, lb), lambda i: (0, 0, i)),
            pl.BlockSpec((1, lb), lambda i: (0, i)),
            pl.BlockSpec((1, lb), lambda i: (0, i)),
        ],
        out_specs=(pl.BlockSpec((width + 16, lb), lambda i: (0, i)), pl.BlockSpec((1, lb), lambda i: (0, i))),
        compiler_params=params(),
        name="weigh",
    )(feats_t, totals, weight, first_row)


def mass_rows(mass):
    hi = mass.astype(BF).astype(F32)
    row = lax.broadcasted_iota(jnp.int32, (16, mass.shape[1]), 0)
    return jnp.where(row == 0, hi, jnp.where(row == 1, mass - hi, 0.0))


def numerators(chunk, lhs, scaled, dtype, lanes, nb=256):
    height, rows = lhs.shape
    width = height - 16

    def kern(chunk_ref, l_ref, a_ref, o_ref):
        out = lax.dot_general(l_ref[...], a_ref[...], NN, preferred_element_type=F32)
        mass = jnp.sum(out[width:], axis=0, keepdims=True)
        o_ref[pl.ds(0, width), :] = out[:width].astype(dtype)
        o_ref[pl.ds(width, 16), :] = mass_rows(mass).astype(dtype)

    per = lanes // nb
    return pl.pallas_call(
        kern,
        out_shape=jax.ShapeDtypeStruct((height, lanes), dtype),
        grid_spec=pltpu.PrefetchScalarGridSpec(
            num_scalar_prefetch=1,
            grid=(per,),
            in_specs=[
                pl.BlockSpec((height, rows), lambda j, chunk: (0, 0)),
                pl.BlockSpec((rows, nb), lambda j, chunk: (0, chunk[0] * per + j)),
            ],
            out_specs=pl.BlockSpec((height, nb), lambda j, chunk: (0, j)),
        ),
        compiler_params=params(),
        name="numerators",
    )(chunk, lhs, scaled)


def add_first(position, own, arrived):
    height, lanes = own.shape
    width = height - 16
    piece = lanes // 4

    def kern(pos_ref, own_ref, r1, r2, r3, *outs):
        for d in range(4):
            at = pl.ds(pl.multiple_of(lax.rem(pos_ref[0] + d, 4) * piece, piece), piece)
            total = own_ref[:, at]
            for r in (r1, r2, r3):
                total = total + r[:, at].astype(F32)
            mass = jnp.sum(total[width:], axis=0, keepdims=True)
            outs[d][pl.ds(0, width), :] = total[:width].astype(outs[d].dtype)
            outs[d][pl.ds(width, 16), :] = mass_rows(mass).astype(outs[d].dtype)

    whole = pl.BlockSpec(memory_space=pltpu.VMEM)
    return pl.pallas_call(
        kern,
        out_shape=[jax.ShapeDtypeStruct((height, piece), F32 if d == 0 else BF) for d in range(4)],
        in_specs=[pl.BlockSpec(memory_space=pltpu.SMEM)] + [whole] * 4,
        out_specs=[whole] * 4,
        compiler_params=params(),
        name="add_first",
    )(position, own, *arrived)


def add_second(own, arrived):
    height, lanes = own.shape
    width = height - 16

    def kern(own_ref, r1, r2, r3, o_ref):
        total = own_ref[...]
        for r in (r1, r2, r3):
            total = total + r[...].astype(F32)
        mass = jnp.sum(total[width:], axis=0, keepdims=True)
        o_ref[...] = (total[:width] / mass).T.astype(BF)

    whole = pl.BlockSpec(memory_space=pltpu.VMEM)
    return pl.pallas_call(
        kern,
        out_shape=jax.ShapeDtypeStruct((lanes, width), BF),
        in_specs=[whole] * 4,
        out_specs=whole,
        compiler_params=params(),
        name="add_second",
    )(own, *arrived)


def per_device(features, codebook):
    me = lax.axis_index("pts")
    core = me % 2
    x, y = me // 8, (me // 2) % 4
    codes = codebook.shape[0] // 2
    total_rows = features.shape[0] * lax.axis_size("pts")
    total_codes = codebook.shape[0] * lax.axis_size("code")
    target = math.log(total_rows / total_codes)
    core_arr = core.astype(jnp.int32).reshape(1)

    theirs = other_core(features)
    lse_own = columns(core_arr, features, codebook, codes)
    lse_their = columns(core_arr, theirs, codebook, codes)
    feats = jnp.where(core == 0, jnp.stack([features, theirs]), jnp.stack([theirs, features]))
    feats = feats.reshape(-1, features.shape[1])
    feats_t = feats.T

    def across(value):
        group = [
            [place(a, b, c) * 4 + z for c in range(2) for z in range(4)]
            for a in range(4) for b in range(4)
        ]
        return lax.all_to_all(value, ("pts", "code"), 0, 0, tiled=True, axis_index_groups=group)

    def around(value, move):
        return [value] + [move(value, d) for d in (1, 2, 3)]

    lse = lse_of(around(lse_of([lse_own, lse_their]), along_x))
    scaled, lses, peak, first_col = rows_first(core_arr, feats, codebook, around(lse, along_y), target, codes)
    sums, first_row, weight = col_sums_first(scaled, across(lses), peak)
    sums = sum(around(sums, along_x))
    totals, _ = row_sums(scaled, weight, around(sums, along_y), first_col, math.exp(target))
    sums = col_sums(scaled, across(totals), weight)
    sums = sum(around(sums, along_x))
    totals, col_pot = row_sums(scaled, weight, around(sums, along_y), first_col, math.exp(target))
    lhs, row_pot = weigh(feats_t, across(totals), weight, first_row)

    at_first = jnp.where(core == 0, y, x)
    at_second = jnp.where(core == 0, x, y)
    their_first = jnp.where(core == 0, x, y)
    quarter = codes // 4

    def chunk(d):
        return ((at_first + d) % 4).astype(jnp.int32).reshape(1)

    arrived = []
    for d in (2, 1, 3):
        arrived.append(first_axis(numerators(chunk(d), lhs, scaled, BF, quarter), d))
    own = numerators(chunk(0), lhs, scaled, F32, quarter)
    pieces = add_first(at_second.astype(jnp.int32).reshape(1), own, arrived)
    arrived = [second_axis(pieces[d], d) for d in (2, 1, 3)]
    fresh = add_second(pieces[0], arrived)

    piece = quarter // 4
    part = jnp.zeros((quarter, fresh.shape[1]), BF)
    for d in range(4):
        got = fresh if d == 0 else second_axis(fresh, d)
        part = lax.dynamic_update_slice(part, got, (((at_second - d) % 4) * piece, 0))
    out = jnp.zeros(codebook.shape, BF)
    for d in (2, 1, 3, 0):
        got = part if d == 0 else first_axis(part, d)
        out = lax.dynamic_update_slice(out, got, (core * codes + ((at_first - d) % 4) * quarter, 0))
        got = other_core(got)
        out = lax.dynamic_update_slice(out, got, ((1 - core) * codes + ((their_first - d) % 4) * quarter, 0))

    half = row_pot.shape[1] // 2
    my_rows = lax.dynamic_slice(row_pot.reshape(-1), (core * half,), (half,))
    their_col = other_core(col_pot)
    cols = jnp.where(core == 0, jnp.stack([col_pot, their_col]), jnp.stack([their_col, col_pot])).reshape(-1)
    return out, my_rows, cols


def solution(mesh):
    return jax.shard_map(
        per_device,
        mesh=mesh,
        in_specs=(P("pts", None), P("code", None)),
        out_specs=(P("code", None), P("pts"), P("code")),
        check_vma=False,
    )
```

```python
import functools
import math

import jax
import jax.numpy as jnp
from jax import lax
from jax.experimental import pallas as pl
from jax.experimental.pallas import tpu as pltpu
from jax.sharding import PartitionSpec as P

BF = jnp.bfloat16
F32 = jnp.float32
NT = (((1,), (1,)), ((), ()))
NN = (((1,), (0,)), ((), ()))


def place(x, y, c):
    return ((x % 4) * 4 + (y % 4)) * 2 + c


def shift(value, move):
    pairs = []
    for x in range(4):
        for y in range(4):
            for c in range(2):
                pairs.append((place(x, y, c), place(*move(x, y, c))))
    return lax.ppermute(value, "pts", pairs)


def along_x(value, d):
    return shift(value, lambda x, y, c: (x + d, y, c))


def along_y(value, d):
    return shift(value, lambda x, y, c: (x, y + d, c))


def other_core(value):
    return shift(value, lambda x, y, c: (x, y, 1 - c))


def first_axis(value, d):
    return shift(value, lambda x, y, c: (x + d * c, y + d * (1 - c), c))


def second_axis(value, d):
    return shift(value, lambda x, y, c: (x + d * (1 - c), y + d * c, c))


def params(mib=32):
    return pltpu.CompilerParams(vmem_limit_bytes=mib * 1024 * 1024)


def lse_of(parts):
    peak = functools.reduce(jnp.maximum, parts)
    return peak + jnp.log(sum(jnp.exp(p - peak) for p in parts))


def split_rows(v):
    n = v.shape[1]
    hi = v.astype(BF).astype(F32)
    mid = (v - hi).astype(BF).astype(F32)
    low = v - hi - mid
    row = lax.broadcasted_iota(jnp.int32, (16, n), 0)
    return jnp.where(row == 0, hi, jnp.where(row == 1, mid, jnp.where(row == 2, low, 0.0))).astype(BF)


def to_row(col):
    n = col.shape[0]
    diag = lax.broadcasted_iota(jnp.int32, (128, 128), 0) == lax.broadcasted_iota(jnp.int32, (128, 128), 1)
    parts = []
    for i in range(0, n, 128):
        parts.append(jnp.sum(jnp.where(diag, col[i : i + 128], 0.0), axis=0, keepdims=True))
    return jnp.concatenate(parts, axis=1)


WHOLE = pl.BlockSpec(memory_space=pltpu.VMEM)
SCALARS = pl.BlockSpec(memory_space=pltpu.SMEM)
ANYWHERE = pl.BlockSpec(memory_space=pl.ANY)


def columns_body(f_ref, c_ref, o_ref, buf, bc, ready=None):
    tiles = c_ref.shape[0] // bc

    def product(j):
        if ready is not None:
            ready(j)
        buf[j % 2] = lax.dot_general(
            f_ref[...], c_ref[j * bc : (j + 1) * bc, :], NT, preferred_element_type=F32
        )

    product(0)
    for j in range(tiles):
        if j + 1 < tiles:
            product(j + 1)
        part = buf.at[j % 2]
        peak = jnp.max(part[...], axis=0, keepdims=True)
        total = jnp.sum(jnp.exp(part[...] - peak), axis=0, keepdims=True)
        o_ref[:, j * bc : (j + 1) * bc] = peak + jnp.log(total)


def columns_first(core, feats, codebook, codes, bc=256):
    rows, width = feats.shape
    tiles = codes // bc

    def kern(core_ref, f_hbm, c_hbm, o_ref, half_ref, f_ref, buf, sems):
        copies = [pltpu.make_async_copy(f_hbm, f_ref, sems.at[tiles])]
        for j in range(tiles):
            start = pl.multiple_of(core_ref[0] * codes + j * bc, bc)
            copies.append(
                pltpu.make_async_copy(
                    c_hbm.at[pl.ds(start, bc), :], half_ref.at[pl.ds(j * bc, bc), :], sems.at[j]
                )
            )
        for c in copies:
            c.start()
        copies[0].wait()
        columns_body(f_ref, half_ref, o_ref, buf, bc, lambda j: copies[j + 1].wait())

    return pl.pallas_call(
        kern,
        out_shape=(jax.ShapeDtypeStruct((1, codes), F32), pltpu.VMEM((codes, width), BF)),
        in_specs=[SCALARS, ANYWHERE, ANYWHERE],
        out_specs=(WHOLE, WHOLE),
        scratch_shapes=[
            pltpu.VMEM((rows, width), BF),
            pltpu.VMEM((2, rows, bc), F32),
            pltpu.SemaphoreType.DMA((tiles + 1,)),
        ],
        compiler_params=params(54),
        name="columns_first",
    )(core, feats, codebook)


def columns(feats, half, bc=256):
    rows = feats.shape[0]

    def kern(f_ref, c_ref, o_ref, buf):
        columns_body(f_ref, c_ref, o_ref, buf, bc)

    return pl.pallas_call(
        kern,
        out_shape=jax.ShapeDtypeStruct((1, half.shape[0]), F32),
        in_specs=[WHOLE, WHOLE],
        out_specs=WHOLE,
        scratch_shapes=[pltpu.VMEM((2, rows, bc), F32)],
        compiler_params=params(),
        name="columns",
    )(feats, half)


def rows_first(feats, half, parts, target, rb=256, cb=512):
    rows, _ = feats.shape
    codes = half.shape[0]
    blocks, tiles = rows // rb, codes // cb
    per = rb // tiles

    def kern(f_ref, c_ref, p0, p1, p2, p3, a_ref, lse_ref, peak_ref, col_ref, buf, kept):
        col_ref[...] = target - lse_of([p0[...], p1[...], p2[...], p3[...]])

        def product(b, j):
            buf[b % 2, :, j * cb : (j + 1) * cb] = lax.dot_general(
                f_ref[b * rb : (b + 1) * rb, :], c_ref[j * cb : (j + 1) * cb, :], NT, preferred_element_type=F32
            )

        def scale(b, j):
            at = pl.ds(j * per, per)
            val = buf[b % 2, at, :] + col_ref[...]
            peak = jnp.max(val, axis=1, keepdims=True)
            ex = jnp.exp(val - peak)
            total = jnp.sum(ex, axis=1, keepdims=True)
            a_ref[b * rb + j * per : b * rb + (j + 1) * per, :] = ex.astype(BF)
            kept[at, 0:1] = peak
            kept[at, 1:2] = peak + jnp.log(total)

        for j in range(tiles):
            product(0, j)
        for b in range(blocks):
            for j in range(tiles):
                if b + 1 < blocks:
                    product(b + 1, j)
                scale(b, j)
            at = slice(b * rb, (b + 1) * rb)
            peak_ref[:, at] = to_row(kept[:, 0:1])
            lse_ref[:, :, at] = jnp.broadcast_to(to_row(kept[:, 1:2])[None], (8, 1, rb))

    return pl.pallas_call(
        kern,
        out_shape=(
            pltpu.VMEM((rows, codes), BF),
            jax.ShapeDtypeStruct((8, 1, rows), F32),
            jax.ShapeDtypeStruct((1, rows), F32),
            jax.ShapeDtypeStruct((1, codes), F32),
        ),
        in_specs=[WHOLE] * 6,
        out_specs=(WHOLE,) * 4,
        scratch_shapes=[pltpu.VMEM((2, rb, codes), F32), pltpu.VMEM((rb, 128), F32)],
        compiler_params=params(),
        name="rows_first",
    )(feats, half, *parts)


def add_rows(lhs, a_ref, s_ref, nb=512):
    for j in range(a_ref.shape[1] // nb):
        at = slice(j * nb, (j + 1) * nb)
        out = lax.dot_general(lhs[...], a_ref[:, at], NN, preferred_element_type=F32)
        s_ref[:, at] = jnp.sum(out, axis=0, keepdims=True)


def col_sums_first(scaled, lses, peak):
    rows, codes = scaled.shape

    def kern(a_ref, l_ref, p_ref, s_ref, r_ref, w_ref, lhs):
        pot = -lse_of([l_ref[k] for k in range(8)])
        weight = jnp.exp(p_ref[...] + pot)
        r_ref[...] = pot
        w_ref[...] = weight
        lhs[...] = split_rows(weight)
        add_rows(lhs, a_ref, s_ref)

    return pl.pallas_call(
        kern,
        out_shape=(
            jax.ShapeDtypeStruct((1, codes), F32),
            jax.ShapeDtypeStruct((1, rows), F32),
            jax.ShapeDtypeStruct((1, rows), F32),
        ),
        in_specs=[WHOLE] * 3,
        out_specs=(WHOLE,) * 3,
        scratch_shapes=[pltpu.VMEM((16, rows), BF)],
        compiler_params=params(20),
        name="col_sums_first",
    )(scaled, lses, peak)


def col_sums(scaled, totals, weight):
    rows, codes = scaled.shape

    def kern(a_ref, t_ref, w_ref, s_ref, lhs):
        lhs[...] = split_rows(w_ref[...] / sum(t_ref[k] for k in range(8)))
        add_rows(lhs, a_ref, s_ref)

    return pl.pallas_call(
        kern,
        out_shape=jax.ShapeDtypeStruct((1, codes), F32),
        in_specs=[WHOLE] * 3,
        out_specs=WHOLE,
        scratch_shapes=[pltpu.VMEM((16, rows), BF)],
        compiler_params=params(20),
        name="col_sums",
    )(scaled, totals, weight)


def row_sums(scaled, weight, parts, first_col, scale, rb=512):
    rows, codes = scaled.shape

    def kern(a_ref, w_ref, p0, p1, p2, p3, c_ref, t_ref, col_ref, lhs):
        ratio = scale / (p0[...] + p1[...] + p2[...] + p3[...])
        col_ref[...] = c_ref[...] + jnp.log(ratio)
        lhs[...] = split_rows(ratio)
        for j in range(rows // rb):
            at = slice(j * rb, (j + 1) * rb)
            out = lax.dot_general(lhs[...], a_ref[at, :], NT, preferred_element_type=F32)
            total = jnp.sum(out, axis=0, keepdims=True) * w_ref[:, at]
            t_ref[:, :, at] = jnp.broadcast_to(total[None], (8, 1, rb))

    return pl.pallas_call(
        kern,
        out_shape=(jax.ShapeDtypeStruct((8, 1, rows), F32), jax.ShapeDtypeStruct((1, codes), F32)),
        in_specs=[WHOLE] * 7,
        out_specs=(WHOLE, WHOLE),
        scratch_shapes=[pltpu.VMEM((16, codes), BF)],
        compiler_params=params(20),
        name="row_sums",
    )(scaled, weight, *parts, first_col)


def weigh(feats_t, totals, weight, first_row):
    width, rows = feats_t.shape

    def kern(f_ref, t_ref, w_ref, r_ref, lhs_ref, row_ref):
        total = sum(t_ref[k] for k in range(8))
        rho = w_ref[...] / total
        row_ref[...] = r_ref[...] - jnp.log(total)
        lhs_ref[pl.ds(0, width), :] = (f_ref[...].astype(F32) * rho).astype(BF)
        lhs_ref[pl.ds(width, 16), :] = split_rows(rho)

    return pl.pallas_call(
        kern,
        out_shape=(pltpu.VMEM((width + 16, rows), BF), jax.ShapeDtypeStruct((1, rows), F32)),
        in_specs=[WHOLE] * 4,
        out_specs=(WHOLE, WHOLE),
        compiler_params=params(20),
        name="weigh",
    )(feats_t, totals, weight, first_row)


def mass_rows(mass):
    hi = mass.astype(BF).astype(F32)
    row = lax.broadcasted_iota(jnp.int32, (16, mass.shape[1]), 0)
    return jnp.where(row == 0, hi, jnp.where(row == 1, mass - hi, 0.0))


def numerators(chunk, lhs, scaled, dtype, lanes):
    height = lhs.shape[0]
    width = height - 16

    def kern(chunk_ref, l_ref, a_ref, o_ref):
        for q in range(scaled.shape[1] // lanes):

            @pl.when(chunk_ref[0] == q)
            def _():
                at = slice(q * lanes, (q + 1) * lanes)
                out = lax.dot_general(l_ref[...], a_ref[:, at], NN, preferred_element_type=F32)
                mass = jnp.sum(out[width:], axis=0, keepdims=True)
                o_ref[pl.ds(0, width), :] = out[:width].astype(dtype)
                o_ref[pl.ds(width, 16), :] = mass_rows(mass).astype(dtype)

    return pl.pallas_call(
        kern,
        out_shape=jax.ShapeDtypeStruct((height, lanes), dtype),
        in_specs=[SCALARS, WHOLE, WHOLE],
        out_specs=WHOLE,
        compiler_params=params(20),
        name="numerators",
    )(chunk, lhs, scaled)


def add_first(position, own, arrived):
    height, lanes = own.shape
    width = height - 16
    piece = lanes // 4

    def kern(pos_ref, own_ref, r1, r2, r3, *outs):
        for d in range(4):
            at = pl.ds(pl.multiple_of(lax.rem(pos_ref[0] + d, 4) * piece, piece), piece)
            total = own_ref[:, at]
            for r in (r1, r2, r3):
                total = total + r[:, at].astype(F32)
            mass = jnp.sum(total[width:], axis=0, keepdims=True)
            outs[d][pl.ds(0, width), :] = total[:width].astype(outs[d].dtype)
            outs[d][pl.ds(width, 16), :] = mass_rows(mass).astype(outs[d].dtype)

    return pl.pallas_call(
        kern,
        out_shape=[jax.ShapeDtypeStruct((height, piece), F32 if d == 0 else BF) for d in range(4)],
        in_specs=[SCALARS] + [WHOLE] * 4,
        out_specs=[WHOLE] * 4,
        compiler_params=params(),
        name="add_first",
    )(position, own, *arrived)


def add_second(own, arrived):
    height, lanes = own.shape
    width = height - 16

    def kern(own_ref, r1, r2, r3, o_ref):
        total = own_ref[...]
        for r in (r1, r2, r3):
            total = total + r[...].astype(F32)
        mass = jnp.sum(total[width:], axis=0, keepdims=True)
        o_ref[...] = (total[:width] / mass).T.astype(BF)

    return pl.pallas_call(
        kern,
        out_shape=jax.ShapeDtypeStruct((lanes, width), BF),
        in_specs=[WHOLE] * 4,
        out_specs=WHOLE,
        compiler_params=params(),
        name="add_second",
    )(own, *arrived)


def assemble(base, shape, pieces, starts):
    count = len(pieces)
    rows = pieces[0].shape[0]
    where = jnp.stack([jnp.asarray(s, jnp.int32) for s in starts])

    def kern(at_ref, *refs):
        sources, o_ref, sems = refs[:count], refs[-2], refs[-1]
        copies = []
        for i in range(count):
            at = pl.ds(pl.multiple_of(at_ref[i], rows), rows)
            copies.append(pltpu.make_async_copy(sources[i], o_ref.at[at, :], sems.at[i]))
        for c in copies:
            c.start()
        for c in copies:
            c.wait()

    given = [] if base is None else [base]
    return pl.pallas_call(
        kern,
        out_shape=jax.ShapeDtypeStruct(shape, pieces[0].dtype),
        in_specs=[SCALARS] + [ANYWHERE] * (count + len(given)),
        out_specs=ANYWHERE,
        scratch_shapes=[pltpu.SemaphoreType.DMA((count,))],
        input_output_aliases={} if base is None else {1 + count: 0},
        compiler_params=params(8),
        name="assemble",
    )(where, *pieces, *given)


def per_device(features, codebook):
    me = lax.axis_index("pts")
    core = me % 2
    x, y = me // 8, (me // 2) % 4
    codes = codebook.shape[0] // 2
    total_rows = features.shape[0] * lax.axis_size("pts")
    total_codes = codebook.shape[0] * lax.axis_size("code")
    target = math.log(total_rows / total_codes)
    core_arr = core.astype(jnp.int32).reshape(1)

    theirs = other_core(features)
    lse_own, half = columns_first(core_arr, features, codebook, codes)
    lse_their = columns(theirs, half)
    feats = jnp.where(core == 0, jnp.stack([features, theirs]), jnp.stack([theirs, features]))
    feats = feats.reshape(-1, features.shape[1])
    feats_t = feats.T

    def across(value):
        group = [
            [place(a, b, c) * 4 + z for c in range(2) for z in range(4)]
            for a in range(4) for b in range(4)
        ]
        return lax.all_to_all(value, ("pts", "code"), 0, 0, tiled=True, axis_index_groups=group)

    def around(value, move):
        return [value] + [move(value, d) for d in (1, 2, 3)]

    lse = lse_of(around(lse_of([lse_own, lse_their]), along_x))
    scaled, lses, peak, first_col = rows_first(feats, half, around(lse, along_y), target)
    sums, first_row, weight = col_sums_first(scaled, across(lses), peak)
    sums = sum(around(sums, along_x))
    totals, _ = row_sums(scaled, weight, around(sums, along_y), first_col, math.exp(target))
    sums = col_sums(scaled, across(totals), weight)
    sums = sum(around(sums, along_x))
    totals, col_pot = row_sums(scaled, weight, around(sums, along_y), first_col, math.exp(target))
    lhs, row_pot = weigh(feats_t, across(totals), weight, first_row)

    at_first = jnp.where(core == 0, y, x)
    at_second = jnp.where(core == 0, x, y)
    their_first = jnp.where(core == 0, x, y)
    quarter = codes // 4

    def chunk(d):
        return ((at_first + d) % 4).astype(jnp.int32).reshape(1)

    arrived = []
    for d in (2, 1, 3):
        arrived.append(first_axis(numerators(chunk(d), lhs, scaled, BF, quarter), d))
    own = numerators(chunk(0), lhs, scaled, F32, quarter)
    pieces = add_first(at_second.astype(jnp.int32).reshape(1), own, arrived)
    arrived = [second_axis(pieces[d], d) for d in (2, 1, 3)]
    fresh = add_second(pieces[0], arrived)

    piece = quarter // 4
    gathered = [fresh] + [second_axis(fresh, d) for d in (1, 2, 3)]
    starts = [((at_second - d) % 4) * piece for d in range(4)]
    part = assemble(None, (quarter, fresh.shape[1]), gathered, starts)
    first = [part] + [first_axis(part, d) for d in (2, 1, 3)]
    starts = [core * codes + ((at_first - d) % 4) * quarter for d in (0, 2, 1, 3)]
    other = [other_core(f) for f in first]
    starts += [(1 - core) * codes + ((their_first - d) % 4) * quarter for d in (0, 2, 1, 3)]
    pieces = first + other
    early, late = (0, 1, 2, 4), (3, 5, 6, 7)
    out = assemble(None, codebook.shape, [pieces[i] for i in early], [starts[i] for i in early])
    out = assemble(out, codebook.shape, [pieces[i] for i in late], [starts[i] for i in late])

    mine = features.shape[0]
    my_rows = lax.dynamic_slice(row_pot.reshape(-1), (core * mine,), (mine,))
    their_col = other_core(col_pot)
    cols = jnp.where(core == 0, jnp.stack([col_pot, their_col]), jnp.stack([their_col, col_pot])).reshape(-1)
    return out, my_rows, cols


def solution(mesh):
    return jax.shard_map(
        per_device,
        mesh=mesh,
        in_specs=(P("pts", None), P("code", None)),
        out_specs=(P("code", None), P("pts"), P("code")),
        check_vma=False,
    )
```

```python
import functools
import math

import jax
import jax.numpy as jnp
from jax import lax
from jax.experimental import pallas as pl
from jax.experimental.pallas import tpu as pltpu
from jax.sharding import PartitionSpec as P

BF = jnp.bfloat16
F32 = jnp.float32
NT = (((1,), (1,)), ((), ()))
NN = (((1,), (0,)), ((), ()))


def place(x, y, c):
    return ((x % 4) * 4 + (y % 4)) * 2 + c


def shift(value, move):
    pairs = []
    for x in range(4):
        for y in range(4):
            for c in range(2):
                pairs.append((place(x, y, c), place(*move(x, y, c))))
    return lax.ppermute(value, "pts", pairs)


def along_x(value, d):
    return shift(value, lambda x, y, c: (x + d, y, c))


def along_y(value, d):
    return shift(value, lambda x, y, c: (x, y + d, c))


def other_core(value):
    return shift(value, lambda x, y, c: (x, y, 1 - c))


def first_axis(value, d):
    return shift(value, lambda x, y, c: (x + d * c, y + d * (1 - c), c))


def second_axis(value, d):
    return shift(value, lambda x, y, c: (x + d * (1 - c), y + d * c, c))


def params(mib=32):
    return pltpu.CompilerParams(vmem_limit_bytes=mib * 1024 * 1024)


def cost(flops):
    return pl.CostEstimate(flops=flops, bytes_accessed=0, transcendentals=0)


def held(value):
    return pltpu.with_memory_space_constraint(value, pltpu.VMEM)


def lse_of(parts):
    peak = functools.reduce(jnp.maximum, parts)
    return peak + jnp.log(sum(jnp.exp(p - peak) for p in parts))


def split_rows(v):
    n = v.shape[1]
    hi = v.astype(BF).astype(F32)
    mid = (v - hi).astype(BF).astype(F32)
    low = v - hi - mid
    row = lax.broadcasted_iota(jnp.int32, (16, n), 0)
    return jnp.where(row == 0, hi, jnp.where(row == 1, mid, jnp.where(row == 2, low, 0.0))).astype(BF)


def to_row(col):
    n = col.shape[0]
    diag = lax.broadcasted_iota(jnp.int32, (128, 128), 0) == lax.broadcasted_iota(jnp.int32, (128, 128), 1)
    parts = []
    for i in range(0, n, 128):
        parts.append(jnp.sum(jnp.where(diag, col[i : i + 128], 0.0), axis=0, keepdims=True))
    return jnp.concatenate(parts, axis=1)


WHOLE = pl.BlockSpec(memory_space=pltpu.VMEM)
SCALARS = pl.BlockSpec(memory_space=pltpu.SMEM)
ANYWHERE = pl.BlockSpec(memory_space=pl.ANY)


def columns_body(f_ref, c_ref, o_ref, buf, bc):
    tiles = c_ref.shape[0] // bc

    def product(j):
        buf[j % 2] = lax.dot_general(
            f_ref[...], c_ref[j * bc : (j + 1) * bc, :], NT, preferred_element_type=F32
        )

    product(0)
    for j in range(tiles):
        if j + 1 < tiles:
            product(j + 1)
        part = buf.at[j % 2]
        peak = jnp.max(part[...], axis=0, keepdims=True)
        total = jnp.sum(jnp.exp(part[...] - peak), axis=0, keepdims=True)
        o_ref[:, j * bc : (j + 1) * bc] = peak + jnp.log(total)


def columns_first(core, feats, codebook, codes, bc=256):
    rows, width = feats.shape
    tiles = codes // bc

    def kern(core_ref, f_hbm, c_hbm, o_ref, half_ref, f_ref, buf, sems):
        copies = [pltpu.make_async_copy(f_hbm, f_ref, sems.at[tiles])]
        for j in range(tiles):
            start = pl.multiple_of(core_ref[0] * codes + j * bc, bc)
            copies.append(
                pltpu.make_async_copy(
                    c_hbm.at[pl.ds(start, bc), :], half_ref.at[pl.ds(j * bc, bc), :], sems.at[j]
                )
            )
        for c in copies:
            c.start()
        for c in copies:
            c.wait()
        columns_body(f_ref, half_ref, o_ref, buf, bc)

    return pl.pallas_call(
        kern,
        out_shape=(jax.ShapeDtypeStruct((1, codes), F32), pltpu.VMEM((codes, width), BF)),
        in_specs=[SCALARS, ANYWHERE, ANYWHERE],
        out_specs=(WHOLE, WHOLE),
        scratch_shapes=[
            pltpu.VMEM((rows, width), BF),
            pltpu.VMEM((2, rows, bc), F32),
            pltpu.SemaphoreType.DMA((tiles + 1,)),
        ],
        compiler_params=params(16),
        name="columns_first",
    )(
        core,
        pltpu.with_memory_space_constraint(feats, pltpu.HBM),
        pltpu.with_memory_space_constraint(codebook, pltpu.HBM),
    )


def columns(feats, half, bc=256):
    rows = feats.shape[0]

    def kern(f_ref, c_ref, o_ref, buf):
        columns_body(f_ref, c_ref, o_ref, buf, bc)

    return pl.pallas_call(
        kern,
        out_shape=jax.ShapeDtypeStruct((1, half.shape[0]), F32),
        in_specs=[WHOLE, WHOLE],
        out_specs=WHOLE,
        scratch_shapes=[pltpu.VMEM((2, rows, bc), F32)],
        compiler_params=params(12),
        name="columns",
    )(feats, held(half))


def ordered(core, own, theirs):
    rows, width = own.shape

    def kern(core_ref, own_ref, their_ref, f_ref, t_ref):
        for h in range(2):

            @pl.when(core_ref[0] == h)
            def _():
                for at, ref in ((h, own_ref), (1 - h, their_ref)):
                    part = ref[...]
                    f_ref[at * rows : (at + 1) * rows, :] = part
                    t_ref[:, at * rows : (at + 1) * rows] = part.T

    return pl.pallas_call(
        kern,
        out_shape=(pltpu.VMEM((2 * rows, width), BF), pltpu.VMEM((width, 2 * rows), BF)),
        in_specs=[SCALARS, WHOLE, WHOLE],
        out_specs=(WHOLE, WHOLE),
        compiler_params=params(12),
        name="ordered",
    )(core, own, theirs)


def rows_first(feats, half, parts, target, rb=256, cb=512):
    rows, _ = feats.shape
    codes = half.shape[0]
    blocks, tiles = rows // rb, codes // cb
    per = rb // tiles

    def kern(f_ref, c_ref, p0, p1, p2, p3, a_ref, lse_ref, peak_ref, col_ref, buf, kept):
        col_ref[...] = target - lse_of([p0[...], p1[...], p2[...], p3[...]])

        def product(b, j):
            buf[b % 2, :, j * cb : (j + 1) * cb] = lax.dot_general(
                f_ref[b * rb : (b + 1) * rb, :], c_ref[j * cb : (j + 1) * cb, :], NT, preferred_element_type=F32
            )

        def scale(b, j):
            at = pl.ds(j * per, per)
            val = buf[b % 2, at, :] + col_ref[...]
            peak = jnp.max(val, axis=1, keepdims=True)
            ex = jnp.exp(val - peak)
            total = jnp.sum(ex, axis=1, keepdims=True)
            a_ref[b * rb + j * per : b * rb + (j + 1) * per, :] = ex.astype(BF)
            kept[at, 0:1] = peak
            kept[at, 1:2] = peak + jnp.log(total)

        for j in range(tiles):
            product(0, j)
        for b in range(blocks):
            for j in range(tiles):
                if b + 1 < blocks:
                    product(b + 1, j)
                scale(b, j)
            at = slice(b * rb, (b + 1) * rb)
            peak_ref[:, at] = to_row(kept[:, 0:1])
            lse_ref[:, :, at] = jnp.broadcast_to(to_row(kept[:, 1:2])[None], (8, 1, rb))

    return pl.pallas_call(
        kern,
        out_shape=(
            pltpu.VMEM((rows, codes), BF),
            jax.ShapeDtypeStruct((8, 1, rows), F32),
            jax.ShapeDtypeStruct((1, rows), F32),
            jax.ShapeDtypeStruct((1, codes), F32),
        ),
        in_specs=[WHOLE] * 6,
        out_specs=(WHOLE,) * 4,
        scratch_shapes=[pltpu.VMEM((2, rb, codes), F32), pltpu.VMEM((rb, 128), F32)],
        compiler_params=params(20),
        name="rows_first",
    )(held(feats), held(half), *parts)


def add_rows(lhs, a_ref, s_ref, nb=512):
    for j in range(a_ref.shape[1] // nb):
        at = slice(j * nb, (j + 1) * nb)
        out = lax.dot_general(lhs[...], a_ref[:, at], NN, preferred_element_type=F32)
        s_ref[:, at] = jnp.sum(out, axis=0, keepdims=True)


def col_sums_first(scaled, lses, peak):
    rows, codes = scaled.shape

    def kern(a_ref, l_ref, p_ref, s_ref, r_ref, w_ref, lhs):
        pot = -lse_of([l_ref[k] for k in range(8)])
        weight = jnp.exp(p_ref[...] + pot)
        r_ref[...] = pot
        w_ref[...] = weight
        lhs[...] = split_rows(weight)
        add_rows(lhs, a_ref, s_ref)

    return pl.pallas_call(
        kern,
        out_shape=(
            jax.ShapeDtypeStruct((1, codes), F32),
            jax.ShapeDtypeStruct((1, rows), F32),
            jax.ShapeDtypeStruct((1, rows), F32),
        ),
        in_specs=[WHOLE] * 3,
        out_specs=(WHOLE,) * 3,
        scratch_shapes=[pltpu.VMEM((16, rows), BF)],
        compiler_params=params(12),
        name="col_sums_first",
    )(held(scaled), lses, peak)


def col_sums(scaled, totals, weight):
    rows, codes = scaled.shape

    def kern(a_ref, t_ref, w_ref, s_ref, lhs):
        lhs[...] = split_rows(w_ref[...] / sum(t_ref[k] for k in range(8)))
        add_rows(lhs, a_ref, s_ref)

    return pl.pallas_call(
        kern,
        out_shape=jax.ShapeDtypeStruct((1, codes), F32),
        in_specs=[WHOLE] * 3,
        out_specs=WHOLE,
        scratch_shapes=[pltpu.VMEM((16, rows), BF)],
        compiler_params=params(12),
        name="col_sums",
    )(held(scaled), totals, weight)


def row_sums(scaled, weight, parts, first_col, scale, rb=512):
    rows, codes = scaled.shape

    def kern(a_ref, w_ref, p0, p1, p2, p3, c_ref, t_ref, col_ref, lhs):
        ratio = scale / (p0[...] + p1[...] + p2[...] + p3[...])
        col_ref[...] = c_ref[...] + jnp.log(ratio)
        lhs[...] = split_rows(ratio)
        for j in range(rows // rb):
            at = slice(j * rb, (j + 1) * rb)
            out = lax.dot_general(lhs[...], a_ref[at, :], NT, preferred_element_type=F32)
            total = jnp.sum(out, axis=0, keepdims=True) * w_ref[:, at]
            t_ref[:, :, at] = jnp.broadcast_to(total[None], (8, 1, rb))

    return pl.pallas_call(
        kern,
        out_shape=(jax.ShapeDtypeStruct((8, 1, rows), F32), jax.ShapeDtypeStruct((1, codes), F32)),
        in_specs=[WHOLE] * 7,
        out_specs=(WHOLE, WHOLE),
        scratch_shapes=[pltpu.VMEM((16, codes), BF)],
        compiler_params=params(12),
        name="row_sums",
    )(held(scaled), weight, *parts, first_col)


def weigh(core, feats_t, totals, weight, first_row):
    width, rows = feats_t.shape

    def kern(core_ref, f_ref, t_ref, w_ref, r_ref, lhs_ref, row_ref):
        total = sum(t_ref[k] for k in range(8))
        rho = w_ref[...] / total
        pot = r_ref[...] - jnp.log(total)
        mine = rows // 2
        row_ref[...] = jnp.where(core_ref[0] == 0, pot[:, :mine], pot[:, mine:])
        lhs_ref[pl.ds(0, width), :] = (f_ref[...].astype(F32) * rho).astype(BF)
        lhs_ref[pl.ds(width, 16), :] = split_rows(rho)

    return pl.pallas_call(
        kern,
        out_shape=(pltpu.VMEM((width + 16, rows), BF), jax.ShapeDtypeStruct((1, rows // 2), F32)),
        in_specs=[SCALARS] + [WHOLE] * 4,
        out_specs=(WHOLE, WHOLE),
        compiler_params=params(16),
        name="weigh",
    )(core, held(feats_t), totals, weight, first_row)


def mass_rows(mass):
    hi = mass.astype(BF).astype(F32)
    row = lax.broadcasted_iota(jnp.int32, (16, mass.shape[1]), 0)
    return jnp.where(row == 0, hi, jnp.where(row == 1, mass - hi, 0.0))


def numerators(places, slot, lhs, scaled, dtype, lanes):
    height = lhs.shape[0]
    width = height - 16

    def kern(chunk_ref, l_ref, a_ref, o_ref):
        for q in range(scaled.shape[1] // lanes):

            @pl.when(chunk_ref[slot] == q)
            def _():
                at = slice(q * lanes, (q + 1) * lanes)
                out = lax.dot_general(l_ref[...], a_ref[:, at], NN, preferred_element_type=F32)
                mass = jnp.sum(out[width:], axis=0, keepdims=True)
                o_ref[pl.ds(0, width), :] = out[:width].astype(dtype)
                o_ref[pl.ds(width, 16), :] = mass_rows(mass).astype(dtype)

    return pl.pallas_call(
        kern,
        out_shape=jax.ShapeDtypeStruct((height, lanes), dtype),
        in_specs=[SCALARS, WHOLE, WHOLE],
        out_specs=WHOLE,
        compiler_params=params(12),
        cost_estimate=cost(1000),
        name="numerators",
    )(places, held(lhs), held(scaled))


def add_first(places, slot, own, arrived):
    height, lanes = own.shape
    width = height - 16
    piece = lanes // 4

    def kern(pos_ref, own_ref, r1, r2, r3, *outs):
        for d in range(4):
            at = pl.ds(pl.multiple_of(lax.rem(pos_ref[slot] + d, 4) * piece, piece), piece)
            total = own_ref[:, at]
            for r in (r1, r2, r3):
                total = total + r[:, at].astype(F32)
            mass = jnp.sum(total[width:], axis=0, keepdims=True)
            outs[d][pl.ds(0, width), :] = total[:width].astype(outs[d].dtype)
            outs[d][pl.ds(width, 16), :] = mass_rows(mass).astype(outs[d].dtype)

    return pl.pallas_call(
        kern,
        out_shape=[jax.ShapeDtypeStruct((height, piece), F32 if d == 0 else BF) for d in range(4)],
        in_specs=[SCALARS] + [WHOLE] * 4,
        out_specs=[WHOLE] * 4,
        compiler_params=params(12),
        name="add_first",
    )(places, own, *arrived)


def add_second(own, arrived):
    height, lanes = own.shape
    width = height - 16

    def kern(own_ref, r1, r2, r3, o_ref):
        total = own_ref[...]
        for r in (r1, r2, r3):
            total = total + r[...].astype(F32)
        mass = jnp.sum(total[width:], axis=0, keepdims=True)
        o_ref[...] = (total[:width] / mass).T.astype(BF)

    return pl.pallas_call(
        kern,
        out_shape=jax.ShapeDtypeStruct((lanes, width), BF),
        in_specs=[WHOLE] * 4,
        out_specs=WHOLE,
        compiler_params=params(12),
        name="add_second",
    )(own, *arrived)


def assemble(base, shape, pieces, places, slots):
    count = len(pieces)
    rows = pieces[0].shape[0]

    def kern(at_ref, *refs):
        sources, o_ref, sems = refs[:count], refs[-2], refs[-1]
        copies = []
        for i in range(count):
            at = pl.ds(pl.multiple_of(at_ref[slots[i]], rows), rows)
            copies.append(pltpu.make_async_copy(sources[i], o_ref.at[at, :], sems.at[i]))
        for c in copies:
            c.start()
        for c in copies:
            c.wait()

    given = [] if base is None else [base]
    return pl.pallas_call(
        kern,
        out_shape=jax.ShapeDtypeStruct(shape, pieces[0].dtype),
        in_specs=[SCALARS] + [WHOLE] * count + [ANYWHERE] * len(given),
        out_specs=ANYWHERE,
        scratch_shapes=[pltpu.SemaphoreType.DMA((count,))],
        input_output_aliases={} if base is None else {1 + count: 0},
        compiler_params=params(8),
        name="assemble",
    )(places, *[held(p) for p in pieces], *given)


def per_device(features, codebook):
    me = lax.axis_index("pts")
    core = me % 2
    x, y = me // 8, (me // 2) % 4
    codes = codebook.shape[0] // 2
    total_rows = features.shape[0] * lax.axis_size("pts")
    total_codes = codebook.shape[0] * lax.axis_size("code")
    target = math.log(total_rows / total_codes)

    at_first, at_second = jnp.where(core == 0, y, x), jnp.where(core == 0, x, y)
    quarter, piece = codes // 4, codes // 16
    places = jnp.stack(
        [core, at_second]
        + [(at_first + d) % 4 for d in range(4)]
        + [((at_second - d) % 4) * piece for d in range(4)]
        + [core * codes + ((at_first - d) % 4) * quarter for d in range(4)]
        + [(1 - core) * codes + ((at_second - d) % 4) * quarter for d in range(4)]
    ).astype(jnp.int32)

    theirs = other_core(features)
    lse_own, half = columns_first(places, features, codebook, codes)
    lse_their = columns(theirs, half)
    feats, feats_t = ordered(places, features, theirs)

    def across(value):
        group = [
            [place(a, b, c) * 4 + z for c in range(2) for z in range(4)]
            for a in range(4) for b in range(4)
        ]
        return lax.all_to_all(value, ("pts", "code"), 0, 0, tiled=True, axis_index_groups=group)

    def around(value, move):
        return [value] + [move(value, d) for d in (1, 2, 3)]

    lse = lse_of(around(lse_of([lse_own, lse_their]), along_x))
    scaled, lses, peak, first_col = rows_first(feats, half, around(lse, along_y), target)
    sums, first_row, weight = col_sums_first(scaled, across(lses), peak)
    sums = sum(around(sums, along_x))
    totals, _ = row_sums(scaled, weight, around(sums, along_y), first_col, math.exp(target))
    sums = col_sums(scaled, across(totals), weight)
    sums = sum(around(sums, along_x))
    totals, col_pot = row_sums(scaled, weight, around(sums, along_y), first_col, math.exp(target))
    totals, col_pot, feats_t = lax.optimization_barrier((across(totals), col_pot, feats_t))
    lhs, row_pot = weigh(places, feats_t, totals, weight, first_row)

    arrived = []
    for d in (2, 1, 3):
        arrived.append(first_axis(numerators(places, 2 + d, lhs, scaled, BF, quarter), d))
    own = numerators(places, 2, lhs, scaled, F32, quarter)
    pieces = add_first(places, 1, own, arrived)
    arrived = [second_axis(pieces[d], d) for d in (2, 1, 3)]
    fresh = add_second(pieces[0], arrived)

    my_rows = row_pot.reshape(-1)
    their_col = other_core(col_pot)
    cols = jnp.where(core == 0, jnp.stack([col_pot, their_col]), jnp.stack([their_col, col_pot])).reshape(-1)
    fresh, my_rows, cols = lax.optimization_barrier((fresh, my_rows, cols))

    gathered = [fresh] + [second_axis(fresh, d) for d in (1, 2, 3)]
    part = assemble(None, (quarter, fresh.shape[1]), gathered, places, (6, 7, 8, 9))
    arriving = {d: first_axis(part, d) for d in (2, 1, 3)}
    out = assemble(None, codebook.shape, [part, other_core(part)], places, (10, 14))
    arriving[3], out = lax.optimization_barrier((arriving[3], out))
    rest = [arriving[d] for d in (2, 1, 3)] + [other_core(arriving[d]) for d in (2, 1, 3)]
    out = assemble(out, codebook.shape, rest, places, (12, 11, 13, 16, 15, 17))
    return out, my_rows, cols


def solution(mesh):
    return jax.shard_map(
        per_device,
        mesh=mesh,
        in_specs=(P("pts", None), P("code", None)),
        out_specs=(P("code", None), P("pts"), P("code")),
        check_vma=False,
    )
```

```python
import functools
import math

import jax
import jax.numpy as jnp
from jax import lax
from jax.experimental import pallas as pl
from jax.experimental.pallas import tpu as pltpu
from jax.sharding import PartitionSpec as P

BF = jnp.bfloat16
F32 = jnp.float32
NT = (((1,), (1,)), ((), ()))
NN = (((1,), (0,)), ((), ()))


def place(x, y, c):
    return ((x % 4) * 4 + (y % 4)) * 2 + c


def shift(value, move):
    pairs = []
    for x in range(4):
        for y in range(4):
            for c in range(2):
                pairs.append((place(x, y, c), place(*move(x, y, c))))
    return lax.ppermute(value, "pts", pairs)


def other_core(value):
    return shift(value, lambda x, y, c: (x, y, 1 - c))


def first_axis(value, d):
    return shift(value, lambda x, y, c: (x + d * c, y + d * (1 - c), c))


def second_axis(value, d):
    return shift(value, lambda x, y, c: (x + d * (1 - c), y + d * c, c))


def params(mib=32):
    return pltpu.CompilerParams(vmem_limit_bytes=mib * 1024 * 1024)


def cost(flops):
    return pl.CostEstimate(flops=flops, bytes_accessed=0, transcendentals=0)


def held(value):
    return pltpu.with_memory_space_constraint(value, pltpu.VMEM)


def lse_of(parts):
    peak = functools.reduce(jnp.maximum, parts)
    return peak + jnp.log(sum(jnp.exp(p - peak) for p in parts))


def split_rows(v):
    n = v.shape[1]
    hi = v.astype(BF).astype(F32)
    mid = (v - hi).astype(BF).astype(F32)
    low = v - hi - mid
    row = lax.broadcasted_iota(jnp.int32, (16, n), 0)
    return jnp.where(row == 0, hi, jnp.where(row == 1, mid, jnp.where(row == 2, low, 0.0))).astype(BF)


def swapped(core_ref, v):
    n = v.shape[1] // 2
    return jnp.where(core_ref[0] == 0, v, jnp.concatenate([v[:, n:], v[:, :n]], axis=1))


def to_row(col):
    n = col.shape[0]
    diag = lax.broadcasted_iota(jnp.int32, (128, 128), 0) == lax.broadcasted_iota(jnp.int32, (128, 128), 1)
    parts = []
    for i in range(0, n, 128):
        parts.append(jnp.sum(jnp.where(diag, col[i : i + 128], 0.0), axis=0, keepdims=True))
    return jnp.concatenate(parts, axis=1)


WHOLE = pl.BlockSpec(memory_space=pltpu.VMEM)
SCALARS = pl.BlockSpec(memory_space=pltpu.SMEM)
ANYWHERE = pl.BlockSpec(memory_space=pl.ANY)


def columns_body(f_ref, c_ref, o_ref, buf, bc):
    tiles = c_ref.shape[0] // bc

    def product(j):
        buf[j % 2] = lax.dot_general(
            f_ref[...], c_ref[j * bc : (j + 1) * bc, :], NT, preferred_element_type=F32
        )

    product(0)
    for j in range(tiles):
        if j + 1 < tiles:
            product(j + 1)
        part = buf.at[j % 2]
        peak = jnp.max(part[...], axis=0, keepdims=True)
        total = jnp.sum(jnp.exp(part[...] - peak), axis=0, keepdims=True)
        o_ref[:, j * bc : (j + 1) * bc] = peak + jnp.log(total)


def columns_first(core, feats, codebook, codes, bc=256):
    rows, width = feats.shape
    tiles = codes // bc

    def kern(core_ref, f_hbm, c_hbm, o_ref, half_ref, f_ref, buf, sems):
        copies = [pltpu.make_async_copy(f_hbm, f_ref, sems.at[tiles])]
        for j in range(tiles):
            start = pl.multiple_of(core_ref[0] * codes + j * bc, bc)
            copies.append(
                pltpu.make_async_copy(
                    c_hbm.at[pl.ds(start, bc), :], half_ref.at[pl.ds(j * bc, bc), :], sems.at[j]
                )
            )
        for c in copies:
            c.start()
        for c in copies:
            c.wait()
        columns_body(f_ref, half_ref, o_ref, buf, bc)

    return pl.pallas_call(
        kern,
        out_shape=(jax.ShapeDtypeStruct((1, codes), F32), pltpu.VMEM((codes, width), BF)),
        in_specs=[SCALARS, ANYWHERE, ANYWHERE],
        out_specs=(WHOLE, WHOLE),
        scratch_shapes=[
            pltpu.VMEM((rows, width), BF),
            pltpu.VMEM((2, rows, bc), F32),
            pltpu.SemaphoreType.DMA((tiles + 1,)),
        ],
        compiler_params=params(16),
        name="columns_first",
    )(
        core,
        pltpu.with_memory_space_constraint(feats, pltpu.HBM),
        pltpu.with_memory_space_constraint(codebook, pltpu.HBM),
    )


def columns(own, theirs, half, lse_own, bc=256):
    rows, width = own.shape
    codes = half.shape[0]

    def kern(own_ref, f_ref, c_ref, first_ref, o_ref, t_ref, lse_ref, buf):
        t_ref[:, :rows] = own_ref[...].T
        t_ref[:, rows:] = f_ref[...].T
        columns_body(f_ref, c_ref, lse_ref, buf, bc)
        lse = lse_of([first_ref[...], lse_ref[...]])
        o_ref[...] = jnp.broadcast_to(lse[None], o_ref.shape)

    return pl.pallas_call(
        kern,
        out_shape=(jax.ShapeDtypeStruct((16, 1, codes), F32), pltpu.VMEM((width, 2 * rows), BF)),
        in_specs=[WHOLE] * 4,
        out_specs=(WHOLE, WHOLE),
        scratch_shapes=[pltpu.VMEM((1, codes), F32), pltpu.VMEM((2, rows, bc), F32)],
        compiler_params=params(12),
        name="columns",
    )(own, theirs, held(half), lse_own)


def rows_first(places, own, theirs, half, lses, target, rb=256, cb=512):
    rows = 2 * own.shape[0]
    codes = half.shape[0]
    blocks, tiles = rows // rb, codes // cb
    per = rb // tiles

    def kern(core_ref, own_ref, their_ref, c_ref, l_ref, a_ref, lse_ref, peak_ref, col_ref, buf, kept, line):
        col_ref[...] = target - lse_of([l_ref[k] for k in range(16)])

        def product(b, j):
            f_ref = own_ref if b < blocks // 2 else their_ref
            at = b % (blocks // 2) * rb
            buf[b % 2, :, j * cb : (j + 1) * cb] = lax.dot_general(
                f_ref[at : at + rb, :], c_ref[j * cb : (j + 1) * cb, :], NT, preferred_element_type=F32
            )

        def scale(b, j):
            at = pl.ds(j * per, per)
            val = buf[b % 2, at, :] + col_ref[...]
            peak = jnp.max(val, axis=1, keepdims=True)
            ex = jnp.exp(val - peak)
            total = jnp.sum(ex, axis=1, keepdims=True)
            a_ref[b * rb + j * per : b * rb + (j + 1) * per, :] = ex.astype(BF)
            kept[at, 0:1] = peak
            kept[at, 1:2] = peak + jnp.log(total)

        for j in range(tiles):
            product(0, j)
        for b in range(blocks):
            for j in range(tiles):
                if b + 1 < blocks:
                    product(b + 1, j)
                scale(b, j)
            at = slice(b * rb, (b + 1) * rb)
            peak_ref[:, at] = to_row(kept[:, 0:1])
            line[:, at] = to_row(kept[:, 1:2])
        lse_ref[...] = jnp.broadcast_to(swapped(core_ref, line[...])[None], lse_ref.shape)

    return pl.pallas_call(
        kern,
        out_shape=(
            pltpu.VMEM((rows, codes), BF),
            jax.ShapeDtypeStruct((8, 1, rows), F32),
            jax.ShapeDtypeStruct((1, rows), F32),
            jax.ShapeDtypeStruct((1, codes), F32),
        ),
        in_specs=[SCALARS] + [WHOLE] * 4,
        out_specs=(WHOLE,) * 4,
        scratch_shapes=[
            pltpu.VMEM((2, rb, codes), F32),
            pltpu.VMEM((rb, 128), F32),
            pltpu.VMEM((1, rows), F32),
        ],
        compiler_params=params(20),
        name="rows_first",
    )(places, own, theirs, held(half), lses)


def add_rows(lhs, a_ref, s_ref, nb=512):
    for j in range(a_ref.shape[1] // nb):
        at = slice(j * nb, (j + 1) * nb)
        out = lax.dot_general(lhs[...], a_ref[:, at], NN, preferred_element_type=F32)
        s_ref[:, :, at] = jnp.broadcast_to(jnp.sum(out, axis=0, keepdims=True)[None], (16, 1, nb))


def col_sums_first(places, scaled, lses, peak):
    rows, codes = scaled.shape

    def kern(core_ref, a_ref, l_ref, p_ref, s_ref, r_ref, w_ref, lhs):
        pot = swapped(core_ref, -lse_of([l_ref[k] for k in range(8)]))
        weight = jnp.exp(p_ref[...] + pot)
        r_ref[...] = pot
        w_ref[...] = weight
        lhs[...] = split_rows(weight)
        add_rows(lhs, a_ref, s_ref)

    return pl.pallas_call(
        kern,
        out_shape=(
            jax.ShapeDtypeStruct((16, 1, codes), F32),
            jax.ShapeDtypeStruct((1, rows), F32),
            jax.ShapeDtypeStruct((1, rows), F32),
        ),
        in_specs=[SCALARS] + [WHOLE] * 3,
        out_specs=(WHOLE,) * 3,
        scratch_shapes=[pltpu.VMEM((16, rows), BF)],
        compiler_params=params(12),
        name="col_sums_first",
    )(places, held(scaled), lses, peak)


def col_sums(places, scaled, totals, weight):
    rows, codes = scaled.shape

    def kern(core_ref, a_ref, t_ref, w_ref, s_ref, lhs):
        lhs[...] = split_rows(w_ref[...] / swapped(core_ref, sum(t_ref[k] for k in range(8))))
        add_rows(lhs, a_ref, s_ref)

    return pl.pallas_call(
        kern,
        out_shape=jax.ShapeDtypeStruct((16, 1, codes), F32),
        in_specs=[SCALARS] + [WHOLE] * 3,
        out_specs=WHOLE,
        scratch_shapes=[pltpu.VMEM((16, rows), BF)],
        compiler_params=params(12),
        name="col_sums",
    )(places, held(scaled), totals, weight)


def row_sums(places, scaled, weight, sums, first_col, scale, rb=512):
    rows, codes = scaled.shape

    def kern(core_ref, a_ref, w_ref, s_ref, c_ref, t_ref, col_ref, lhs, line):
        ratio = scale / sum(s_ref[k] for k in range(16))
        col_ref[...] = c_ref[...] + jnp.log(ratio)
        lhs[...] = split_rows(ratio)
        for j in range(rows // rb):
            at = slice(j * rb, (j + 1) * rb)
            out = lax.dot_general(lhs[...], a_ref[at, :], NT, preferred_element_type=F32)
            line[:, at] = jnp.sum(out, axis=0, keepdims=True) * w_ref[:, at]
        t_ref[...] = jnp.broadcast_to(swapped(core_ref, line[...])[None], t_ref.shape)

    return pl.pallas_call(
        kern,
        out_shape=(jax.ShapeDtypeStruct((8, 1, rows), F32), jax.ShapeDtypeStruct((1, codes), F32)),
        in_specs=[SCALARS] + [WHOLE] * 4,
        out_specs=(WHOLE, WHOLE),
        scratch_shapes=[pltpu.VMEM((16, codes), BF), pltpu.VMEM((1, rows), F32)],
        compiler_params=params(12),
        name="row_sums",
    )(places, held(scaled), weight, sums, first_col)


def weigh(places, feats_t, totals, weight, first_row):
    width, rows = feats_t.shape

    def kern(core_ref, f_ref, t_ref, w_ref, r_ref, lhs_ref, row_ref):
        total = swapped(core_ref, sum(t_ref[k] for k in range(8)))
        rho = w_ref[...] / total
        row_ref[...] = (r_ref[...] - jnp.log(total))[:, : rows // 2]
        lhs_ref[pl.ds(0, width), :] = (f_ref[...].astype(F32) * rho).astype(BF)
        lhs_ref[pl.ds(width, 16), :] = split_rows(rho)

    return pl.pallas_call(
        kern,
        out_shape=(pltpu.VMEM((width + 16, rows), BF), jax.ShapeDtypeStruct((1, rows // 2), F32)),
        in_specs=[SCALARS] + [WHOLE] * 4,
        out_specs=(WHOLE, WHOLE),
        compiler_params=params(16),
        name="weigh",
    )(places, held(feats_t), totals, weight, first_row)


def mass_rows(mass):
    hi = mass.astype(BF).astype(F32)
    row = lax.broadcasted_iota(jnp.int32, (16, mass.shape[1]), 0)
    return jnp.where(row == 0, hi, jnp.where(row == 1, mass - hi, 0.0))


def numerators(places, slot, lhs, scaled, dtype, lanes):
    height = lhs.shape[0]
    width = height - 16

    def kern(chunk_ref, l_ref, a_ref, o_ref):
        for q in range(scaled.shape[1] // lanes):

            @pl.when(chunk_ref[slot] == q)
            def _():
                at = slice(q * lanes, (q + 1) * lanes)
                out = lax.dot_general(l_ref[...], a_ref[:, at], NN, preferred_element_type=F32)
                mass = jnp.sum(out[width:], axis=0, keepdims=True)
                o_ref[pl.ds(0, width), :] = out[:width].astype(dtype)
                o_ref[pl.ds(width, 16), :] = mass_rows(mass).astype(dtype)

    return pl.pallas_call(
        kern,
        out_shape=jax.ShapeDtypeStruct((height, lanes), dtype),
        in_specs=[SCALARS, WHOLE, WHOLE],
        out_specs=WHOLE,
        compiler_params=params(12),
        cost_estimate=cost(1000),
        name="numerators",
    )(places, held(lhs), held(scaled))


def add_first(places, slot, own, arrived):
    height, lanes = own.shape
    width = height - 16
    piece = lanes // 4

    def kern(pos_ref, own_ref, r1, r2, r3, *outs):
        for d in range(4):
            at = pl.ds(pl.multiple_of(lax.rem(pos_ref[slot] + d, 4) * piece, piece), piece)
            total = own_ref[:, at]
            for r in (r1, r2, r3):
                total = total + r[:, at].astype(F32)
            mass = jnp.sum(total[width:], axis=0, keepdims=True)
            outs[d][pl.ds(0, width), :] = total[:width].astype(outs[d].dtype)
            outs[d][pl.ds(width, 16), :] = mass_rows(mass).astype(outs[d].dtype)

    return pl.pallas_call(
        kern,
        out_shape=[jax.ShapeDtypeStruct((height, piece), F32 if d == 0 else BF) for d in range(4)],
        in_specs=[SCALARS] + [WHOLE] * 4,
        out_specs=[WHOLE] * 4,
        compiler_params=params(12),
        name="add_first",
    )(places, own, *arrived)


def add_second(own, arrived):
    height, lanes = own.shape
    width = height - 16

    def kern(own_ref, r1, r2, r3, o_ref):
        total = own_ref[...]
        for r in (r1, r2, r3):
            total = total + r[...].astype(F32)
        mass = jnp.sum(total[width:], axis=0, keepdims=True)
        o_ref[...] = (total[:width] / mass).T.astype(BF)

    return pl.pallas_call(
        kern,
        out_shape=jax.ShapeDtypeStruct((lanes, width), BF),
        in_specs=[WHOLE] * 4,
        out_specs=WHOLE,
        compiler_params=params(12),
        name="add_second",
    )(own, *arrived)


def pair(upper, lower):
    rows, width = upper.shape

    def kern(u_ref, l_ref, o_ref):
        o_ref[:rows, :] = u_ref[...]
        o_ref[rows:, :] = l_ref[...]

    return pl.pallas_call(
        kern,
        out_shape=jax.ShapeDtypeStruct((2 * rows, width), upper.dtype),
        in_specs=[WHOLE] * 2,
        out_specs=WHOLE,
        compiler_params=params(8),
        name="pair",
    )(upper, lower)


def assemble(base, shape, pairs, places):
    count = len(pairs)
    rows = pairs[0][0].shape[0] // 2

    def kern(at_ref, *refs):
        o_ref, sems = refs[-2], refs[-1]
        copies = []
        for i, (_, chunk, halves) in enumerate(pairs):
            for h in range(2):
                at = pl.ds(pl.multiple_of(at_ref[chunk] + at_ref[halves[h]], rows), rows)
                copies.append(
                    pltpu.make_async_copy(refs[i].at[pl.ds(h * rows, rows), :], o_ref.at[at, :], sems.at[2 * i + h])
                )
        for c in copies:
            c.start()
        for c in copies:
            c.wait()

    given = [] if base is None else [base]
    return pl.pallas_call(
        kern,
        out_shape=jax.ShapeDtypeStruct(shape, pairs[0][0].dtype),
        in_specs=[SCALARS] + [WHOLE] * count + [ANYWHERE] * len(given),
        out_specs=ANYWHERE,
        scratch_shapes=[pltpu.SemaphoreType.DMA((2 * count,))],
        input_output_aliases={} if base is None else {1 + count: 0},
        compiler_params=params(8),
        name="assemble",
    )(places, *[held(p) for p, _, _ in pairs], *given)


def per_device(features, codebook):
    me = lax.axis_index("pts")
    core = me % 2
    x, y = me // 8, (me // 2) % 4
    codes = codebook.shape[0] // 2
    total_rows = features.shape[0] * lax.axis_size("pts")
    total_codes = codebook.shape[0] * lax.axis_size("code")
    target = math.log(total_rows / total_codes)

    at_first, at_second = jnp.where(core == 0, y, x), jnp.where(core == 0, x, y)
    quarter, piece = codes // 4, codes // 16
    places = jnp.stack(
        [core, at_second]
        + [(at_first + d) % 4 for d in range(4)]
        + [core * codes + ((at_first - d) % 4) * quarter for d in range(4)]
        + [((at_second - d) % 4) * piece for d in range(4)]
        + [(1 - core) * codes + ((at_second - d) % 4) * quarter for d in range(4)]
        + [((at_first - d) % 4) * piece for d in range(4)]
    ).astype(jnp.int32)

    theirs = other_core(features)
    lse_own, half = columns_first(places, features, codebook, codes)
    lse, feats_t = columns(features, theirs, half, lse_own)

    def over_chips(value):
        group = [[place(a, b, c) for a in range(4) for b in range(4)] for c in range(2)]
        return lax.all_to_all(value, "pts", 0, 0, tiled=True, axis_index_groups=group)

    def across(value):
        group = [
            [place(a, b, c) * 4 + z for c in range(2) for z in range(4)]
            for a in range(4) for b in range(4)
        ]
        return lax.all_to_all(value, ("pts", "code"), 0, 0, tiled=True, axis_index_groups=group)

    scale = math.exp(target)
    scaled, lses, peak, first_col = rows_first(places, features, theirs, half, over_chips(lse), target)
    sums, first_row, weight = col_sums_first(places, scaled, across(lses), peak)
    totals, _ = row_sums(places, scaled, weight, over_chips(sums), first_col, scale)
    sums = col_sums(places, scaled, across(totals), weight)
    totals, col_pot = row_sums(places, scaled, weight, over_chips(sums), first_col, scale)
    totals, col_pot, feats_t = lax.optimization_barrier((across(totals), col_pot, feats_t))
    lhs, row_pot = weigh(places, feats_t, totals, weight, first_row)

    arrived = []
    for d in (2, 1, 3):
        arrived.append(first_axis(numerators(places, 2 + d, lhs, scaled, BF, quarter), d))
    own = numerators(places, 2, lhs, scaled, F32, quarter)
    pieces = add_first(places, 1, own, arrived)
    arrived = [second_axis(pieces[d], d) for d in (2, 1, 3)]
    fresh = add_second(pieces[0], arrived)

    my_rows = row_pot.reshape(-1)
    their_col = other_core(col_pot)
    cols = jnp.where(core == 0, jnp.stack([col_pot, their_col]), jnp.stack([their_col, col_pot])).reshape(-1)
    fresh, my_rows, cols = lax.optimization_barrier((fresh, my_rows, cols))

    one, three, two = [second_axis(fresh, d) for d in (1, 3, 2)]
    near, far = pair(fresh, one), pair(three, two)

    def placed(value, back, kind):
        halves = (0, 1) if kind == 0 else (3, 2)
        return [
            (value, 6 + back, tuple(10 + d for d in halves)),
            (other_core(value), 14 + back, tuple(18 + d for d in halves)),
        ]

    near_1, far_3 = first_axis(near, 1), first_axis(far, 3)
    far_1, near_3 = first_axis(far, 1), first_axis(near, 3)
    near_2, far_2 = first_axis(near_1, 1), first_axis(far_3, 3)
    out = assemble(None, codebook.shape, placed(near, 0, 0) + placed(far, 0, 1), places)
    near_2, out = lax.optimization_barrier((near_2, out))
    middle = placed(near_1, 1, 0) + placed(far_3, 3, 1) + placed(far_1, 1, 1) + placed(near_3, 3, 0)
    out = assemble(out, codebook.shape, middle, places)
    out = assemble(out, codebook.shape, placed(near_2, 2, 0) + placed(far_2, 2, 1), places)
    return out, my_rows, cols


def solution(mesh):
    return jax.shard_map(
        per_device,
        mesh=mesh,
        in_specs=(P("pts", None), P("code", None)),
        out_specs=(P("code", None), P("pts"), P("code")),
        check_vma=False,
    )
```

```python
import functools
import math

import jax
import jax.numpy as jnp
from jax import lax
from jax.experimental import pallas as pl
from jax.experimental.pallas import tpu as pltpu
from jax.sharding import PartitionSpec as P

BF = jnp.bfloat16
F32 = jnp.float32
NT = (((1,), (1,)), ((), ()))
NN = (((1,), (0,)), ((), ()))


def place(x, y, c):
    return ((x % 4) * 4 + (y % 4)) * 2 + c


def shift(value, move):
    pairs = []
    for x in range(4):
        for y in range(4):
            for c in range(2):
                pairs.append((place(x, y, c), place(*move(x, y, c))))
    return lax.ppermute(value, "pts", pairs)


def other_core(value):
    return shift(value, lambda x, y, c: (x, y, 1 - c))


def first_axis(value, d):
    return shift(value, lambda x, y, c: (x + d * c, y + d * (1 - c), c))


def second_axis(value, d):
    return shift(value, lambda x, y, c: (x + d * (1 - c), y + d * c, c))


def params(mib=32):
    return pltpu.CompilerParams(vmem_limit_bytes=mib * 1024 * 1024)


def cost(flops):
    return pl.CostEstimate(flops=flops, bytes_accessed=0, transcendentals=0)


def held(value):
    return pltpu.with_memory_space_constraint(value, pltpu.VMEM)


def lse_of(parts):
    peak = functools.reduce(jnp.maximum, parts)
    return peak + jnp.log(sum(jnp.exp(p - peak) for p in parts))


def split_rows(v):
    n = v.shape[1]
    hi = v.astype(BF).astype(F32)
    mid = (v - hi).astype(BF).astype(F32)
    low = v - hi - mid
    row = lax.broadcasted_iota(jnp.int32, (16, n), 0)
    return jnp.where(row == 0, hi, jnp.where(row == 1, mid, jnp.where(row == 2, low, 0.0))).astype(BF)


def coordinates(me_ref):
    me = me_ref[0]
    core, y, x = me & 1, (me >> 1) & 3, me >> 3
    return core, jnp.where(core == 0, y, x), jnp.where(core == 0, x, y)


def to_block(line):
    return jnp.concatenate([line[:, i : i + 128] for i in range(0, line.shape[1], 128)], axis=0)


def to_line(block):
    return jnp.concatenate([block[i : i + 1] for i in range(block.shape[0])], axis=1)


def swapped(me_ref, block):
    n = block.shape[0] // 2
    return jnp.where(coordinates(me_ref)[0] == 0, block, jnp.concatenate([block[n:], block[:n]], axis=0))


def copies_of(count, n):
    return jax.ShapeDtypeStruct((count, n // 128, 128), F32)


def block_of(n):
    return jax.ShapeDtypeStruct((n // 128, 128), F32)


def to_row(col):
    n = col.shape[0]
    diag = lax.broadcasted_iota(jnp.int32, (128, 128), 0) == lax.broadcasted_iota(jnp.int32, (128, 128), 1)
    parts = []
    for i in range(0, n, 128):
        parts.append(jnp.sum(jnp.where(diag, col[i : i + 128], 0.0), axis=0, keepdims=True))
    return jnp.concatenate(parts, axis=1)


WHOLE = pl.BlockSpec(memory_space=pltpu.VMEM)
SCALARS = pl.BlockSpec(memory_space=pltpu.SMEM)
ANYWHERE = pl.BlockSpec(memory_space=pl.ANY)


def columns_body(f_ref, c_ref, o_ref, buf, bc):
    tiles = c_ref.shape[0] // bc

    def product(j):
        buf[j % 2] = lax.dot_general(
            f_ref[...], c_ref[j * bc : (j + 1) * bc, :], NT, preferred_element_type=F32
        )

    product(0)
    for j in range(tiles):
        if j + 1 < tiles:
            product(j + 1)
        part = buf.at[j % 2]
        peak = jnp.max(part[...], axis=0, keepdims=True)
        total = jnp.sum(jnp.exp(part[...] - peak), axis=0, keepdims=True)
        o_ref[:, j * bc : (j + 1) * bc] = peak + jnp.log(total)


def columns_first(me, feats, codebook, codes, bc=256):
    rows, width = feats.shape
    tiles = codes // bc

    def kern(me_ref, f_hbm, c_hbm, o_ref, half_ref, f_ref, line, buf, sems):
        copies = [pltpu.make_async_copy(f_hbm, f_ref, sems.at[tiles])]
        for j in range(tiles):
            start = pl.multiple_of(coordinates(me_ref)[0] * codes + j * bc, bc)
            copies.append(
                pltpu.make_async_copy(
                    c_hbm.at[pl.ds(start, bc), :], half_ref.at[pl.ds(j * bc, bc), :], sems.at[j]
                )
            )
        for c in copies:
            c.start()
        for c in copies:
            c.wait()
        columns_body(f_ref, half_ref, line, buf, bc)
        o_ref[...] = to_block(line[...])

    return pl.pallas_call(
        kern,
        out_shape=(block_of(codes), pltpu.VMEM((codes, width), BF)),
        in_specs=[SCALARS, ANYWHERE, ANYWHERE],
        out_specs=(WHOLE, WHOLE),
        scratch_shapes=[
            pltpu.VMEM((rows, width), BF),
            pltpu.VMEM((1, codes), F32),
            pltpu.VMEM((2, rows, bc), F32),
            pltpu.SemaphoreType.DMA((tiles + 1,)),
        ],
        compiler_params=params(16),
        name="columns_first",
    )(
        me,
        pltpu.with_memory_space_constraint(feats, pltpu.HBM),
        pltpu.with_memory_space_constraint(codebook, pltpu.HBM),
    )


def columns(own, theirs, half, lse_own, bc=256):
    rows, width = own.shape
    codes = half.shape[0]

    def kern(own_ref, f_ref, c_ref, first_ref, o_ref, t_ref, lse_ref, buf):
        t_ref[:, :rows] = own_ref[...].T
        t_ref[:, rows:] = f_ref[...].T
        columns_body(f_ref, c_ref, lse_ref, buf, bc)
        lse = lse_of([first_ref[...], to_block(lse_ref[...])])
        o_ref[...] = jnp.broadcast_to(lse[None], o_ref.shape)

    return pl.pallas_call(
        kern,
        out_shape=(copies_of(16, codes), pltpu.VMEM((width, 2 * rows), BF)),
        in_specs=[WHOLE] * 4,
        out_specs=(WHOLE, WHOLE),
        scratch_shapes=[pltpu.VMEM((1, codes), F32), pltpu.VMEM((2, rows, bc), F32)],
        compiler_params=params(12),
        name="columns",
    )(own, theirs, held(half), lse_own)


def rows_first(me, own, theirs, half, lses, target, rb=256, cb=512):
    rows = 2 * own.shape[0]
    codes = half.shape[0]
    blocks, tiles = rows // rb, codes // cb
    per = rb // tiles

    def kern(me_ref, own_ref, their_ref, c_ref, l_ref, a_ref, lse_ref, peak_ref, out_ref, buf, kept, line, peak_line, col_ref):
        out_ref[...] = target - lse_of([l_ref[k] for k in range(16)])
        col_ref[...] = to_line(out_ref[...])

        def product(b, j):
            f_ref = own_ref if b < blocks // 2 else their_ref
            at = b % (blocks // 2) * rb
            buf[b % 2, :, j * cb : (j + 1) * cb] = lax.dot_general(
                f_ref[at : at + rb, :], c_ref[j * cb : (j + 1) * cb, :], NT, preferred_element_type=F32
            )

        def scale(b, j):
            at = pl.ds(j * per, per)
            val = buf[b % 2, at, :] + col_ref[...]
            peak = jnp.max(val, axis=1, keepdims=True)
            ex = jnp.exp(val - peak)
            total = jnp.sum(ex, axis=1, keepdims=True)
            a_ref[b * rb + j * per : b * rb + (j + 1) * per, :] = ex.astype(BF)
            kept[at, 0:1] = peak
            kept[at, 1:2] = peak + jnp.log(total)

        for j in range(tiles):
            product(0, j)
        for b in range(blocks):
            for j in range(tiles):
                if b + 1 < blocks:
                    product(b + 1, j)
                scale(b, j)
            at = slice(b * rb, (b + 1) * rb)
            peak_line[:, at] = to_row(kept[:, 0:1])
            line[:, at] = to_row(kept[:, 1:2])
        peak_ref[...] = to_block(peak_line[...])
        lse_ref[...] = jnp.broadcast_to(swapped(me_ref, to_block(line[...]))[None], lse_ref.shape)

    return pl.pallas_call(
        kern,
        out_shape=(
            pltpu.VMEM((rows, codes), BF),
            copies_of(8, rows),
            block_of(rows),
            block_of(codes),
        ),
        in_specs=[SCALARS] + [WHOLE] * 4,
        out_specs=(WHOLE,) * 4,
        scratch_shapes=[
            pltpu.VMEM((2, rb, codes), F32),
            pltpu.VMEM((rb, 128), F32),
            pltpu.VMEM((1, rows), F32),
            pltpu.VMEM((1, rows), F32),
            pltpu.VMEM((1, codes), F32),
        ],
        compiler_params=params(20),
        name="rows_first",
    )(me, own, theirs, held(half), lses)


def add_rows(lhs, a_ref, s_ref, line, nb=512):
    for j in range(a_ref.shape[1] // nb):
        at = slice(j * nb, (j + 1) * nb)
        out = lax.dot_general(lhs[...], a_ref[:, at], NN, preferred_element_type=F32)
        line[:, at] = jnp.sum(out, axis=0, keepdims=True)
    s_ref[...] = jnp.broadcast_to(to_block(line[...])[None], s_ref.shape)


def col_sums_first(me, scaled, lses, peak):
    rows, codes = scaled.shape

    def kern(me_ref, a_ref, l_ref, p_ref, s_ref, r_ref, w_ref, lhs, line):
        pot = swapped(me_ref, -lse_of([l_ref[k] for k in range(8)]))
        weight = jnp.exp(p_ref[...] + pot)
        r_ref[...] = pot
        w_ref[...] = weight
        lhs[...] = split_rows(to_line(weight))
        add_rows(lhs, a_ref, s_ref, line)

    return pl.pallas_call(
        kern,
        out_shape=(
            copies_of(16, codes),
            block_of(rows),
            block_of(rows),
        ),
        in_specs=[SCALARS] + [WHOLE] * 3,
        out_specs=(WHOLE,) * 3,
        scratch_shapes=[pltpu.VMEM((16, rows), BF), pltpu.VMEM((1, codes), F32)],
        compiler_params=params(12),
        name="col_sums_first",
    )(me, held(scaled), lses, peak)


def col_sums(me, scaled, totals, weight):
    rows, codes = scaled.shape

    def kern(me_ref, a_ref, t_ref, w_ref, s_ref, lhs, line):
        lhs[...] = split_rows(to_line(w_ref[...] / swapped(me_ref, sum(t_ref[k] for k in range(8)))))
        add_rows(lhs, a_ref, s_ref, line)

    return pl.pallas_call(
        kern,
        out_shape=copies_of(16, codes),
        in_specs=[SCALARS] + [WHOLE] * 3,
        out_specs=WHOLE,
        scratch_shapes=[pltpu.VMEM((16, rows), BF), pltpu.VMEM((1, codes), F32)],
        compiler_params=params(12),
        name="col_sums",
    )(me, held(scaled), totals, weight)


def row_sums(me, scaled, weight, sums, first_col, scale, rb=512):
    rows, codes = scaled.shape

    def kern(me_ref, a_ref, w_ref, s_ref, c_ref, t_ref, col_ref, lhs, line):
        ratio = scale / sum(s_ref[k] for k in range(16))
        col_ref[...] = c_ref[...] + jnp.log(ratio)
        lhs[...] = split_rows(to_line(ratio))
        for j in range(rows // rb):
            at = slice(j * rb, (j + 1) * rb)
            out = lax.dot_general(lhs[...], a_ref[at, :], NT, preferred_element_type=F32)
            line[:, at] = jnp.sum(out, axis=0, keepdims=True)
        total = to_block(line[...]) * w_ref[...]
        t_ref[...] = jnp.broadcast_to(swapped(me_ref, total)[None], t_ref.shape)

    return pl.pallas_call(
        kern,
        out_shape=(copies_of(8, rows), block_of(codes)),
        in_specs=[SCALARS] + [WHOLE] * 4,
        out_specs=(WHOLE, WHOLE),
        scratch_shapes=[pltpu.VMEM((16, codes), BF), pltpu.VMEM((1, rows), F32)],
        compiler_params=params(12),
        name="row_sums",
    )(me, held(scaled), weight, sums, first_col)


def weigh(me, feats_t, totals, weight, first_row):
    width, rows = feats_t.shape

    def kern(me_ref, f_ref, t_ref, w_ref, r_ref, lhs_ref, row_ref):
        total = swapped(me_ref, sum(t_ref[k] for k in range(8)))
        rho = to_line(w_ref[...] / total)
        row_ref[...] = (r_ref[...] - jnp.log(total))[: rows // 256]
        lhs_ref[pl.ds(0, width), :] = (f_ref[...].astype(F32) * rho).astype(BF)
        lhs_ref[pl.ds(width, 16), :] = split_rows(rho)

    return pl.pallas_call(
        kern,
        out_shape=(pltpu.VMEM((width + 16, rows), BF), block_of(rows // 2)),
        in_specs=[SCALARS] + [WHOLE] * 4,
        out_specs=(WHOLE, WHOLE),
        compiler_params=params(16),
        name="weigh",
    )(me, held(feats_t), totals, weight, first_row)


def mass_rows(mass):
    hi = mass.astype(BF).astype(F32)
    row = lax.broadcasted_iota(jnp.int32, (16, mass.shape[1]), 0)
    return jnp.where(row == 0, hi, jnp.where(row == 1, mass - hi, 0.0))


def numerators(me, distance, lhs, scaled, dtype, lanes):
    height = lhs.shape[0]
    width = height - 16

    def kern(me_ref, l_ref, a_ref, o_ref):
        chunk = (coordinates(me_ref)[1] + distance) & 3
        for q in range(scaled.shape[1] // lanes):

            @pl.when(chunk == q)
            def _():
                at = slice(q * lanes, (q + 1) * lanes)
                out = lax.dot_general(l_ref[...], a_ref[:, at], NN, preferred_element_type=F32)
                mass = jnp.sum(out[width:], axis=0, keepdims=True)
                o_ref[pl.ds(0, width), :] = out[:width].astype(dtype)
                o_ref[pl.ds(width, 16), :] = mass_rows(mass).astype(dtype)

    return pl.pallas_call(
        kern,
        out_shape=jax.ShapeDtypeStruct((height, lanes), dtype),
        in_specs=[SCALARS, WHOLE, WHOLE],
        out_specs=WHOLE,
        compiler_params=params(12),
        cost_estimate=cost(1000),
        name="numerators",
    )(me, held(lhs), held(scaled))


def add_first(me, own, arrived):
    height, lanes = own.shape
    width = height - 16
    piece = lanes // 4

    def kern(me_ref, own_ref, r1, r2, r3, *outs):
        for d in range(4):
            at = pl.ds(pl.multiple_of(((coordinates(me_ref)[2] + d) & 3) * piece, piece), piece)
            total = own_ref[:, at]
            for r in (r1, r2, r3):
                total = total + r[:, at].astype(F32)
            mass = jnp.sum(total[width:], axis=0, keepdims=True)
            outs[d][pl.ds(0, width), :] = total[:width].astype(outs[d].dtype)
            outs[d][pl.ds(width, 16), :] = mass_rows(mass).astype(outs[d].dtype)

    return pl.pallas_call(
        kern,
        out_shape=[jax.ShapeDtypeStruct((height, piece), F32 if d == 0 else BF) for d in range(4)],
        in_specs=[SCALARS] + [WHOLE] * 4,
        out_specs=[WHOLE] * 4,
        compiler_params=params(12),
        name="add_first",
    )(me, own, *arrived)


def add_second(own, arrived):
    height, lanes = own.shape
    width = height - 16

    def kern(own_ref, r1, r2, r3, o_ref):
        total = own_ref[...]
        for r in (r1, r2, r3):
            total = total + r[...].astype(F32)
        mass = jnp.sum(total[width:], axis=0, keepdims=True)
        o_ref[...] = (total[:width] / mass).T.astype(BF)

    return pl.pallas_call(
        kern,
        out_shape=jax.ShapeDtypeStruct((lanes, width), BF),
        in_specs=[WHOLE] * 4,
        out_specs=WHOLE,
        compiler_params=params(12),
        name="add_second",
    )(own, *arrived)


def pair(upper, lower):
    rows, width = upper.shape

    def kern(u_ref, l_ref, o_ref):
        o_ref[:rows, :] = u_ref[...]
        o_ref[rows:, :] = l_ref[...]

    return pl.pallas_call(
        kern,
        out_shape=jax.ShapeDtypeStruct((2 * rows, width), upper.dtype),
        in_specs=[WHOLE] * 2,
        out_specs=WHOLE,
        compiler_params=params(8),
        name="pair",
    )(upper, lower)


def assemble(base, shape, pairs, me):
    count = len(pairs)
    rows = pairs[0][0].shape[0] // 2

    def kern(me_ref, *refs):
        core, first, second = coordinates(me_ref)
        o_ref, sems = refs[-2], refs[-1]
        copies = []
        for i, (_, other, back, halves) in enumerate(pairs):
            a, b, c = (1 - core, second, first) if other else (core, first, second)
            for h in range(2):
                index = a * 16 + ((b - back) & 3) * 4 + ((c - halves[h]) & 3)
                at = pl.ds(pl.multiple_of(index * rows, rows), rows)
                copies.append(
                    pltpu.make_async_copy(refs[i].at[pl.ds(h * rows, rows), :], o_ref.at[at, :], sems.at[2 * i + h])
                )
        for c in copies:
            c.start()
        for c in copies:
            c.wait()

    given = [] if base is None else [base]
    return pl.pallas_call(
        kern,
        out_shape=jax.ShapeDtypeStruct(shape, pairs[0][0].dtype),
        in_specs=[SCALARS] + [WHOLE] * count + [ANYWHERE] * len(given),
        out_specs=ANYWHERE,
        scratch_shapes=[pltpu.SemaphoreType.DMA((2 * count,))],
        input_output_aliases={} if base is None else {1 + count: 0},
        compiler_params=params(8),
        name="assemble",
    )(me, *[held(p) for p, _, _, _ in pairs], *given)


def per_device(features, codebook):
    me = lax.axis_index("pts").astype(jnp.int32).reshape(1)
    codes = codebook.shape[0] // 2
    total_rows = features.shape[0] * lax.axis_size("pts")
    total_codes = codebook.shape[0] * lax.axis_size("code")
    target = math.log(total_rows / total_codes)

    theirs = other_core(features)
    lse_own, half = columns_first(me, features, codebook, codes)
    lse, feats_t = columns(features, theirs, half, lse_own)

    def over_chips(value):
        group = [[place(a, b, c) for a in range(4) for b in range(4)] for c in range(2)]
        return lax.all_to_all(value, "pts", 0, 0, tiled=True, axis_index_groups=group)

    def across(value):
        group = [
            [place(a, b, c) * 4 + z for c in range(2) for z in range(4)]
            for a in range(4) for b in range(4)
        ]
        return lax.all_to_all(value, ("pts", "code"), 0, 0, tiled=True, axis_index_groups=group)

    scale = math.exp(target)
    scaled, lses, peak, first_col = rows_first(me, features, theirs, half, over_chips(lse), target)
    sums, first_row, weight = col_sums_first(me, scaled, across(lses), peak)
    totals, _ = row_sums(me, scaled, weight, over_chips(sums), first_col, scale)
    sums = col_sums(me, scaled, across(totals), weight)
    totals, col_pot = row_sums(me, scaled, weight, over_chips(sums), first_col, scale)
    totals, col_pot, feats_t = lax.optimization_barrier((across(totals), col_pot, feats_t))
    lhs, row_pot = weigh(me, feats_t, totals, weight, first_row)

    arrived = []
    for d in (2, 1, 3):
        arrived.append(first_axis(numerators(me, d, lhs, scaled, BF, codes // 4), d))
    own = numerators(me, 0, lhs, scaled, F32, codes // 4)
    pieces = add_first(me, own, arrived)
    arrived = [second_axis(pieces[d], d) for d in (2, 1, 3)]
    fresh = add_second(pieces[0], arrived)

    my_rows = row_pot.reshape(-1)
    their_col = other_core(col_pot)
    cols = jnp.where(me[0] & 1 == 0, jnp.stack([col_pot, their_col]), jnp.stack([their_col, col_pot])).reshape(-1)
    fresh, my_rows, cols = lax.optimization_barrier((fresh, my_rows, cols))

    one, three, two = [second_axis(fresh, d) for d in (1, 3, 2)]
    near, far = pair(fresh, one), pair(three, two)

    def placed(value, back, kind):
        halves = (0, 1) if kind == 0 else (3, 2)
        return [
            (value, False, back, halves),
            (other_core(value), True, back, halves),
        ]

    near_1, far_3 = first_axis(near, 1), first_axis(far, 3)
    far_1, near_3 = first_axis(far, 1), first_axis(near, 3)
    near_2, far_2 = first_axis(near_1, 1), first_axis(far_3, 3)
    out = assemble(None, codebook.shape, placed(near, 0, 0) + placed(far, 0, 1), me)
    near_2, out = lax.optimization_barrier((near_2, out))
    middle = placed(near_1, 1, 0) + placed(far_3, 3, 1) + placed(far_1, 1, 1) + placed(near_3, 3, 0)
    out = assemble(out, codebook.shape, middle, me)
    out = assemble(out, codebook.shape, placed(near_2, 2, 0) + placed(far_2, 2, 1), me)
    return out, my_rows, cols


def solution(mesh):
    return jax.shard_map(
        per_device,
        mesh=mesh,
        in_specs=(P("pts", None), P("code", None)),
        out_specs=(P("code", None), P("pts"), P("code")),
        check_vma=False,
    )
```

```python
import functools
import math

import jax
import jax.numpy as jnp
from jax import lax
from jax.experimental import pallas as pl
from jax.experimental.pallas import tpu as pltpu
from jax.sharding import PartitionSpec as P

BF = jnp.bfloat16
F32 = jnp.float32
NT = (((1,), (1,)), ((), ()))
NN = (((1,), (0,)), ((), ()))


def place(x, y, c):
    return ((x % 4) * 4 + (y % 4)) * 2 + c


def shift(value, move):
    pairs = []
    for x in range(4):
        for y in range(4):
            for c in range(2):
                pairs.append((place(x, y, c), place(*move(x, y, c))))
    return lax.ppermute(value, "pts", pairs)


def other_core(value):
    return shift(value, lambda x, y, c: (x, y, 1 - c))


def first_axis(value, d):
    return shift(value, lambda x, y, c: (x + d * c, y + d * (1 - c), c))


def second_axis(value, d):
    return shift(value, lambda x, y, c: (x + d * (1 - c), y + d * c, c))


def params(mib=32):
    return pltpu.CompilerParams(vmem_limit_bytes=mib * 1024 * 1024)


def cost(flops):
    return pl.CostEstimate(flops=flops, bytes_accessed=0, transcendentals=0)


def held(value):
    return pltpu.with_memory_space_constraint(value, pltpu.VMEM)


def lse_of(parts):
    peak = functools.reduce(jnp.maximum, parts)
    return peak + jnp.log(sum(jnp.exp(p - peak) for p in parts))


def split_rows(v):
    n = v.shape[1]
    hi = v.astype(BF).astype(F32)
    mid = (v - hi).astype(BF).astype(F32)
    low = v - hi - mid
    row = lax.broadcasted_iota(jnp.int32, (16, n), 0)
    return jnp.where(row == 0, hi, jnp.where(row == 1, mid, jnp.where(row == 2, low, 0.0))).astype(BF)


def coordinates(me_ref):
    me = me_ref[0]
    core, y, x = me & 1, (me >> 1) & 3, me >> 3
    return core, jnp.where(core == 0, y, x), jnp.where(core == 0, x, y)


def to_block(line):
    return jnp.concatenate([line[:, i : i + 128] for i in range(0, line.shape[1], 128)], axis=0)


def to_line(block):
    return jnp.concatenate([block[i : i + 1] for i in range(block.shape[0])], axis=1)


def swapped(me_ref, block):
    n = block.shape[0] // 2
    return jnp.where(coordinates(me_ref)[0] == 0, block, jnp.concatenate([block[n:], block[:n]], axis=0))


def copies_of(count, n):
    return jax.ShapeDtypeStruct((count, n // 128, 128), F32)


def block_of(n):
    return jax.ShapeDtypeStruct((n // 128, 128), F32)


def to_row(col):
    n = col.shape[0]
    diag = lax.broadcasted_iota(jnp.int32, (128, 128), 0) == lax.broadcasted_iota(jnp.int32, (128, 128), 1)
    parts = []
    for i in range(0, n, 128):
        parts.append(jnp.sum(jnp.where(diag, col[i : i + 128], 0.0), axis=0, keepdims=True))
    return jnp.concatenate(parts, axis=1)


WHOLE = pl.BlockSpec(memory_space=pltpu.VMEM)
SCALARS = pl.BlockSpec(memory_space=pltpu.SMEM)
ANYWHERE = pl.BlockSpec(memory_space=pl.ANY)


def columns_body(f_ref, c_ref, o_ref, buf, bc, first=0, last=None):
    last = c_ref.shape[0] // bc if last is None else last

    def product(j):
        buf[j % 2] = lax.dot_general(
            f_ref[...], c_ref[j * bc : (j + 1) * bc, :], NT, preferred_element_type=F32
        )

    product(first)
    for j in range(first, last):
        if j + 1 < last:
            product(j + 1)
        part = buf.at[j % 2]
        peak = jnp.max(part[...], axis=0, keepdims=True)
        total = jnp.sum(jnp.exp(part[...] - peak), axis=0, keepdims=True)
        o_ref[:, j * bc : (j + 1) * bc] = peak + jnp.log(total)


def columns_first(me, feats, codebook, codes, bc=256):
    rows, width = feats.shape
    tiles = codes // bc

    def kern(me_ref, f_hbm, c_hbm, o_ref, half_ref, f_ref, line, buf, sems):
        copies = [pltpu.make_async_copy(f_hbm, f_ref, sems.at[tiles])]
        for j in range(tiles):
            start = pl.multiple_of(coordinates(me_ref)[0] * codes + j * bc, bc)
            copies.append(
                pltpu.make_async_copy(
                    c_hbm.at[pl.ds(start, bc), :], half_ref.at[pl.ds(j * bc, bc), :], sems.at[j]
                )
            )
        for c in copies:
            c.start()
        middle = tiles // 4
        for c in copies[: 1 + middle]:
            c.wait()
        columns_body(f_ref, half_ref, line, buf, bc, 0, middle)
        for c in copies[1 + middle :]:
            c.wait()
        columns_body(f_ref, half_ref, line, buf, bc, middle, tiles)
        o_ref[...] = to_block(line[...])

    return pl.pallas_call(
        kern,
        out_shape=(block_of(codes), pltpu.VMEM((codes, width), BF)),
        in_specs=[SCALARS, ANYWHERE, ANYWHERE],
        out_specs=(WHOLE, WHOLE),
        scratch_shapes=[
            pltpu.VMEM((rows, width), BF),
            pltpu.VMEM((1, codes), F32),
            pltpu.VMEM((2, rows, bc), F32),
            pltpu.SemaphoreType.DMA((tiles + 1,)),
        ],
        compiler_params=params(16),
        name="columns_first",
    )(
        me,
        pltpu.with_memory_space_constraint(feats, pltpu.HBM),
        pltpu.with_memory_space_constraint(codebook, pltpu.HBM),
    )


def columns(own, theirs, half, lse_own, bc=256):
    rows, width = own.shape
    codes = half.shape[0]

    def kern(own_ref, f_ref, c_ref, first_ref, o_ref, t_ref, lse_ref, buf):
        t_ref[:, :rows] = own_ref[...].T
        t_ref[:, rows:] = f_ref[...].T
        columns_body(f_ref, c_ref, lse_ref, buf, bc)
        lse = lse_of([first_ref[...], to_block(lse_ref[...])])
        o_ref[...] = jnp.broadcast_to(lse[None], o_ref.shape)

    return pl.pallas_call(
        kern,
        out_shape=(copies_of(16, codes), pltpu.VMEM((width, 2 * rows), BF)),
        in_specs=[WHOLE] * 4,
        out_specs=(WHOLE, WHOLE),
        scratch_shapes=[pltpu.VMEM((1, codes), F32), pltpu.VMEM((2, rows, bc), F32)],
        compiler_params=params(12),
        name="columns",
    )(own, theirs, held(half), lse_own)


def rows_first(me, own, theirs, half, lses, target, rb=256, cb=512):
    rows = 2 * own.shape[0]
    codes = half.shape[0]
    blocks, tiles = rows // rb, codes // cb
    per = rb // tiles

    def kern(me_ref, own_ref, their_ref, c_ref, l_ref, a_ref, lse_ref, peak_ref, out_ref, buf, kept, line, peak_line, col_ref):
        out_ref[...] = target - lse_of([l_ref[k] for k in range(16)])
        col_ref[...] = to_line(out_ref[...])

        def product(b, j):
            f_ref = own_ref if b < blocks // 2 else their_ref
            at = b % (blocks // 2) * rb
            buf[b % 2, :, j * cb : (j + 1) * cb] = lax.dot_general(
                f_ref[at : at + rb, :], c_ref[j * cb : (j + 1) * cb, :], NT, preferred_element_type=F32
            )

        def scale(b, j):
            at = pl.ds(j * per, per)
            val = buf[b % 2, at, :] + col_ref[...]
            peak = jnp.max(val, axis=1, keepdims=True)
            ex = jnp.exp(val - peak)
            total = jnp.sum(ex, axis=1, keepdims=True)
            a_ref[b * rb + j * per : b * rb + (j + 1) * per, :] = ex.astype(BF)
            kept[at, 0:1] = peak
            kept[at, 1:2] = peak + jnp.log(total)

        for j in range(tiles):
            product(0, j)
        for b in range(blocks):
            for j in range(tiles):
                if b + 1 < blocks:
                    product(b + 1, j)
                scale(b, j)
            at = slice(b * rb, (b + 1) * rb)
            peak_line[:, at] = to_row(kept[:, 0:1])
            line[:, at] = to_row(kept[:, 1:2])
        peak_ref[...] = to_block(peak_line[...])
        lse_ref[...] = jnp.broadcast_to(swapped(me_ref, to_block(line[...]))[None], lse_ref.shape)

    return pl.pallas_call(
        kern,
        out_shape=(
            pltpu.VMEM((rows, codes), BF),
            copies_of(8, rows),
            block_of(rows),
            block_of(codes),
        ),
        in_specs=[SCALARS] + [WHOLE] * 4,
        out_specs=(WHOLE,) * 4,
        scratch_shapes=[
            pltpu.VMEM((2, rb, codes), F32),
            pltpu.VMEM((rb, 128), F32),
            pltpu.VMEM((1, rows), F32),
            pltpu.VMEM((1, rows), F32),
            pltpu.VMEM((1, codes), F32),
        ],
        compiler_params=params(20),
        name="rows_first",
    )(me, own, theirs, held(half), lses)


def add_rows(lhs, a_ref, s_ref, line, nb=512):
    for j in range(a_ref.shape[1] // nb):
        at = slice(j * nb, (j + 1) * nb)
        out = lax.dot_general(lhs[...], a_ref[:, at], NN, preferred_element_type=F32)
        line[:, at] = jnp.sum(out, axis=0, keepdims=True)
    s_ref[...] = jnp.broadcast_to(to_block(line[...])[None], s_ref.shape)


def col_sums_first(me, scaled, lses, peak):
    rows, codes = scaled.shape

    def kern(me_ref, a_ref, l_ref, p_ref, s_ref, r_ref, w_ref, lhs, line):
        pot = swapped(me_ref, -lse_of([l_ref[k] for k in range(8)]))
        weight = jnp.exp(p_ref[...] + pot)
        r_ref[...] = pot
        w_ref[...] = weight
        lhs[...] = split_rows(to_line(weight))
        add_rows(lhs, a_ref, s_ref, line)

    return pl.pallas_call(
        kern,
        out_shape=(
            copies_of(16, codes),
            block_of(rows),
            block_of(rows),
        ),
        in_specs=[SCALARS] + [WHOLE] * 3,
        out_specs=(WHOLE,) * 3,
        scratch_shapes=[pltpu.VMEM((16, rows), BF), pltpu.VMEM((1, codes), F32)],
        compiler_params=params(12),
        name="col_sums_first",
    )(me, held(scaled), lses, peak)


def col_sums(me, scaled, totals, weight):
    rows, codes = scaled.shape

    def kern(me_ref, a_ref, t_ref, w_ref, s_ref, lhs, line):
        lhs[...] = split_rows(to_line(w_ref[...] / swapped(me_ref, sum(t_ref[k] for k in range(8)))))
        add_rows(lhs, a_ref, s_ref, line)

    return pl.pallas_call(
        kern,
        out_shape=copies_of(16, codes),
        in_specs=[SCALARS] + [WHOLE] * 3,
        out_specs=WHOLE,
        scratch_shapes=[pltpu.VMEM((16, rows), BF), pltpu.VMEM((1, codes), F32)],
        compiler_params=params(12),
        name="col_sums",
    )(me, held(scaled), totals, weight)


def row_sums(me, scaled, weight, sums, first_col, scale, rb=512):
    rows, codes = scaled.shape

    def kern(me_ref, a_ref, w_ref, s_ref, c_ref, t_ref, col_ref, lhs, line):
        ratio = scale / sum(s_ref[k] for k in range(16))
        col_ref[...] = c_ref[...] + jnp.log(ratio)
        lhs[...] = split_rows(to_line(ratio))
        for j in range(rows // rb):
            at = slice(j * rb, (j + 1) * rb)
            out = lax.dot_general(lhs[...], a_ref[at, :], NT, preferred_element_type=F32)
            line[:, at] = jnp.sum(out, axis=0, keepdims=True)
        total = to_block(line[...]) * w_ref[...]
        t_ref[...] = jnp.broadcast_to(swapped(me_ref, total)[None], t_ref.shape)

    return pl.pallas_call(
        kern,
        out_shape=(copies_of(8, rows), block_of(codes)),
        in_specs=[SCALARS] + [WHOLE] * 4,
        out_specs=(WHOLE, WHOLE),
        scratch_shapes=[pltpu.VMEM((16, codes), BF), pltpu.VMEM((1, rows), F32)],
        compiler_params=params(12),
        name="row_sums",
    )(me, held(scaled), weight, sums, first_col)


def weigh(me, feats_t, totals, weight, first_row):
    width, rows = feats_t.shape

    def kern(me_ref, f_ref, t_ref, w_ref, r_ref, lhs_ref, row_ref):
        total = swapped(me_ref, sum(t_ref[k] for k in range(8)))
        rho = to_line(w_ref[...] / total)
        row_ref[...] = (r_ref[...] - jnp.log(total))[: rows // 256]
        lhs_ref[pl.ds(0, width), :] = (f_ref[...].astype(F32) * rho).astype(BF)
        lhs_ref[pl.ds(width, 16), :] = split_rows(rho)

    return pl.pallas_call(
        kern,
        out_shape=(pltpu.VMEM((width + 16, rows), BF), block_of(rows // 2)),
        in_specs=[SCALARS] + [WHOLE] * 4,
        out_specs=(WHOLE, WHOLE),
        compiler_params=params(16),
        name="weigh",
    )(me, held(feats_t), totals, weight, first_row)


def mass_rows(mass):
    hi = mass.astype(BF).astype(F32)
    row = lax.broadcasted_iota(jnp.int32, (16, mass.shape[1]), 0)
    return jnp.where(row == 0, hi, jnp.where(row == 1, mass - hi, 0.0))


def numerators(me, distance, lhs, scaled, dtype, lanes):
    height = lhs.shape[0]
    width = height - 16

    def kern(me_ref, l_ref, a_ref, o_ref):
        chunk = (coordinates(me_ref)[1] + distance) & 3
        for q in range(scaled.shape[1] // lanes):

            @pl.when(chunk == q)
            def _():
                at = slice(q * lanes, (q + 1) * lanes)
                out = lax.dot_general(l_ref[...], a_ref[:, at], NN, preferred_element_type=F32)
                mass = jnp.sum(out[width:], axis=0, keepdims=True)
                o_ref[pl.ds(0, width), :] = out[:width].astype(dtype)
                o_ref[pl.ds(width, 16), :] = mass_rows(mass).astype(dtype)

    return pl.pallas_call(
        kern,
        out_shape=jax.ShapeDtypeStruct((height, lanes), dtype),
        in_specs=[SCALARS, WHOLE, WHOLE],
        out_specs=WHOLE,
        compiler_params=params(12),
        cost_estimate=cost(1000),
        name="numerators",
    )(me, held(lhs), held(scaled))


def add_first(me, own, arrived):
    height, lanes = own.shape
    width = height - 16
    piece = lanes // 4

    def kern(me_ref, own_ref, r1, r2, r3, *outs):
        for d in range(4):
            at = pl.ds(pl.multiple_of(((coordinates(me_ref)[2] + d) & 3) * piece, piece), piece)
            total = own_ref[:, at]
            for r in (r1, r2, r3):
                total = total + r[:, at].astype(F32)
            mass = jnp.sum(total[width:], axis=0, keepdims=True)
            outs[d][pl.ds(0, width), :] = total[:width].astype(outs[d].dtype)
            outs[d][pl.ds(width, 16), :] = mass_rows(mass).astype(outs[d].dtype)

    return pl.pallas_call(
        kern,
        out_shape=[jax.ShapeDtypeStruct((height, piece), F32 if d == 0 else BF) for d in range(4)],
        in_specs=[SCALARS] + [WHOLE] * 4,
        out_specs=[WHOLE] * 4,
        compiler_params=params(12),
        name="add_first",
    )(me, own, *arrived)


def add_second(own, arrived):
    height, lanes = own.shape
    width = height - 16

    def kern(own_ref, r1, r2, r3, o_ref):
        total = own_ref[...]
        for r in (r1, r2, r3):
            total = total + r[...].astype(F32)
        mass = jnp.sum(total[width:], axis=0, keepdims=True)
        o_ref[...] = (total[:width] / mass).T.astype(BF)

    return pl.pallas_call(
        kern,
        out_shape=jax.ShapeDtypeStruct((lanes, width), BF),
        in_specs=[WHOLE] * 4,
        out_specs=WHOLE,
        compiler_params=params(12),
        name="add_second",
    )(own, *arrived)


def pair(upper, lower):
    rows, width = upper.shape

    def kern(u_ref, l_ref, o_ref):
        o_ref[:rows, :] = u_ref[...]
        o_ref[rows:, :] = l_ref[...]

    return pl.pallas_call(
        kern,
        out_shape=jax.ShapeDtypeStruct((2 * rows, width), upper.dtype),
        in_specs=[WHOLE] * 2,
        out_specs=WHOLE,
        compiler_params=params(8),
        name="pair",
    )(upper, lower)


def assemble(base, shape, pairs, me):
    count = len(pairs)
    rows = pairs[0][0].shape[0] // 2

    def kern(me_ref, *refs):
        core, first, second = coordinates(me_ref)
        o_ref, sems = refs[-2], refs[-1]
        copies = []
        for i, (_, other, back, halves) in enumerate(pairs):
            a, b, c = (1 - core, second, first) if other else (core, first, second)
            for h in range(2):
                index = a * 16 + ((b - back) & 3) * 4 + ((c - halves[h]) & 3)
                at = pl.ds(pl.multiple_of(index * rows, rows), rows)
                copies.append(
                    pltpu.make_async_copy(refs[i].at[pl.ds(h * rows, rows), :], o_ref.at[at, :], sems.at[2 * i + h])
                )
        for c in copies:
            c.start()
        for c in copies:
            c.wait()

    given = [] if base is None else [base]
    return pl.pallas_call(
        kern,
        out_shape=jax.ShapeDtypeStruct(shape, pairs[0][0].dtype),
        in_specs=[SCALARS] + [WHOLE] * count + [ANYWHERE] * len(given),
        out_specs=ANYWHERE,
        scratch_shapes=[pltpu.SemaphoreType.DMA((2 * count,))],
        input_output_aliases={} if base is None else {1 + count: 0},
        compiler_params=params(8),
        name="assemble",
    )(me, *[held(p) for p, _, _, _ in pairs], *given)


def per_device(features, codebook):
    me = lax.axis_index("pts").astype(jnp.int32).reshape(1)
    codes = codebook.shape[0] // 2
    total_rows = features.shape[0] * lax.axis_size("pts")
    total_codes = codebook.shape[0] * lax.axis_size("code")
    target = math.log(total_rows / total_codes)

    theirs = other_core(features)
    lse_own, half = columns_first(me, features, codebook, codes)
    lse, feats_t = columns(features, theirs, half, lse_own)

    def over_chips(value):
        group = [[place(a, b, c) for a in range(4) for b in range(4)] for c in range(2)]
        return lax.all_to_all(value, "pts", 0, 0, tiled=True, axis_index_groups=group)

    def across(value):
        group = [
            [place(a, b, c) * 4 + z for c in range(2) for z in range(4)]
            for a in range(4) for b in range(4)
        ]
        return lax.all_to_all(value, ("pts", "code"), 0, 0, tiled=True, axis_index_groups=group)

    scale = math.exp(target)
    scaled, lses, peak, first_col = rows_first(me, features, theirs, half, over_chips(lse), target)
    sums, first_row, weight = col_sums_first(me, scaled, across(lses), peak)
    totals, _ = row_sums(me, scaled, weight, over_chips(sums), first_col, scale)
    sums = col_sums(me, scaled, across(totals), weight)
    totals, col_pot = row_sums(me, scaled, weight, over_chips(sums), first_col, scale)
    totals, col_pot, feats_t = lax.optimization_barrier((across(totals), col_pot, feats_t))
    lhs, row_pot = weigh(me, feats_t, totals, weight, first_row)

    arrived = []
    for d in (3, 1, 2):
        arrived.append(first_axis(numerators(me, d, lhs, scaled, BF, codes // 4), d))
    own = numerators(me, 0, lhs, scaled, F32, codes // 4)
    pieces = add_first(me, own, arrived)
    arrived = [second_axis(pieces[d], d) for d in (2, 1, 3)]
    fresh = add_second(pieces[0], arrived)

    my_rows = row_pot.reshape(-1)
    their_col = other_core(col_pot)
    cols = jnp.where(me[0] & 1 == 0, jnp.stack([col_pot, their_col]), jnp.stack([their_col, col_pot])).reshape(-1)
    fresh, my_rows, cols = lax.optimization_barrier((fresh, my_rows, cols))

    one, three, two = lax.optimization_barrier(tuple(second_axis(fresh, d) for d in (1, 3, 2)))
    near, far = pair(fresh, one), pair(three, two)

    def placed(value, back, kind):
        halves = (0, 1) if kind == 0 else (3, 2)
        return [
            (value, False, back, halves),
            (other_core(value), True, back, halves),
        ]

    near_1, far_3 = first_axis(near, 1), first_axis(far, 3)
    far_1, near_3 = first_axis(far, 1), first_axis(near, 3)
    near_2, far_2 = first_axis(near_1, 1), first_axis(far_3, 3)
    out = assemble(None, codebook.shape, placed(near, 0, 0) + placed(far, 0, 1), me)
    near_2, out = lax.optimization_barrier((near_2, out))
    middle = placed(near_1, 1, 0) + placed(far_3, 3, 1) + placed(far_1, 1, 1) + placed(near_3, 3, 0)
    out = assemble(out, codebook.shape, middle, me)
    out = assemble(out, codebook.shape, placed(near_2, 2, 0) + placed(far_2, 2, 1), me)
    return out, my_rows, cols


def solution(mesh):
    return jax.shard_map(
        per_device,
        mesh=mesh,
        in_specs=(P("pts", None), P("code", None)),
        out_specs=(P("code", None), P("pts"), P("code")),
        check_vma=False,
    )
```

```python
import functools
import math

import jax
import jax.numpy as jnp
from jax import lax
from jax.experimental import pallas as pl
from jax.experimental.pallas import tpu as pltpu
from jax.sharding import PartitionSpec as P

BF = jnp.bfloat16
F32 = jnp.float32
NT = (((1,), (1,)), ((), ()))
NN = (((1,), (0,)), ((), ()))


def place(x, y, c):
    return ((x % 4) * 4 + (y % 4)) * 2 + c


def shift(value, move):
    pairs = []
    for x in range(4):
        for y in range(4):
            for c in range(2):
                pairs.append((place(x, y, c), place(*move(x, y, c))))
    return lax.ppermute(value, "pts", pairs)


def other_core(value):
    return shift(value, lambda x, y, c: (x, y, 1 - c))


def first_axis(value, d):
    return shift(value, lambda x, y, c: (x + d * c, y + d * (1 - c), c))


def second_axis(value, d):
    return shift(value, lambda x, y, c: (x + d * (1 - c), y + d * c, c))


def params(mib=32):
    return pltpu.CompilerParams(vmem_limit_bytes=mib * 1024 * 1024)


def cost(flops):
    return pl.CostEstimate(flops=flops, bytes_accessed=0, transcendentals=0)


def held(value):
    return pltpu.with_memory_space_constraint(value, pltpu.VMEM)


def lse_of(parts):
    peak = functools.reduce(jnp.maximum, parts)
    return peak + jnp.log(sum(jnp.exp(p - peak) for p in parts))


def split_rows(v):
    n = v.shape[1]
    hi = v.astype(BF).astype(F32)
    mid = (v - hi).astype(BF).astype(F32)
    low = v - hi - mid
    row = lax.broadcasted_iota(jnp.int32, (16, n), 0)
    return jnp.where(row == 0, hi, jnp.where(row == 1, mid, jnp.where(row == 2, low, 0.0))).astype(BF)


def coordinates(me_ref):
    me = me_ref[0]
    core, y, x = me & 1, (me >> 1) & 3, me >> 3
    return core, jnp.where(core == 0, y, x), jnp.where(core == 0, x, y)


def to_block(line):
    return jnp.concatenate([line[:, i : i + 128] for i in range(0, line.shape[1], 128)], axis=0)


def to_line(block):
    return jnp.concatenate([block[i : i + 1] for i in range(block.shape[0])], axis=1)


def swapped(me_ref, block):
    n = block.shape[0] // 2
    return jnp.where(coordinates(me_ref)[0] == 0, block, jnp.concatenate([block[n:], block[:n]], axis=0))


def copies_of(count, n):
    return jax.ShapeDtypeStruct((count, n // 128, 128), F32)


def block_of(n):
    return jax.ShapeDtypeStruct((n // 128, 128), F32)


def to_row(col):
    n = col.shape[0]
    diag = lax.broadcasted_iota(jnp.int32, (128, 128), 0) == lax.broadcasted_iota(jnp.int32, (128, 128), 1)
    parts = []
    for i in range(0, n, 128):
        parts.append(jnp.sum(jnp.where(diag, col[i : i + 128], 0.0), axis=0, keepdims=True))
    return jnp.concatenate(parts, axis=1)


WHOLE = pl.BlockSpec(memory_space=pltpu.VMEM)
SCALARS = pl.BlockSpec(memory_space=pltpu.SMEM)
ANYWHERE = pl.BlockSpec(memory_space=pl.ANY)


def columns_body(f_ref, c_ref, o_ref, buf, bc, first=0, last=None):
    last = c_ref.shape[0] // bc if last is None else last

    def product(j):
        buf[j % 2] = lax.dot_general(
            f_ref[...], c_ref[j * bc : (j + 1) * bc, :], NT, preferred_element_type=F32
        )

    product(first)
    for j in range(first, last):
        if j + 1 < last:
            product(j + 1)
        part = buf.at[j % 2]
        peak = jnp.max(part[...], axis=0, keepdims=True)
        total = jnp.sum(jnp.exp(part[...] - peak), axis=0, keepdims=True)
        o_ref[:, j * bc : (j + 1) * bc] = peak + jnp.log(total)


def columns_first(me, feats, codebook, codes, bc=256):
    rows, width = feats.shape
    tiles = codes // bc

    def kern(me_ref, f_hbm, c_hbm, o_ref, half_ref, f_ref, line, buf, sems):
        copies = [pltpu.make_async_copy(f_hbm, f_ref, sems.at[tiles])]
        for j in range(tiles):
            start = pl.multiple_of(coordinates(me_ref)[0] * codes + j * bc, bc)
            copies.append(
                pltpu.make_async_copy(
                    c_hbm.at[pl.ds(start, bc), :], half_ref.at[pl.ds(j * bc, bc), :], sems.at[j]
                )
            )
        for c in copies:
            c.start()
        middle = tiles // 4
        for c in copies[: 1 + middle]:
            c.wait()
        columns_body(f_ref, half_ref, line, buf, bc, 0, middle)
        for c in copies[1 + middle :]:
            c.wait()
        columns_body(f_ref, half_ref, line, buf, bc, middle, tiles)
        o_ref[...] = to_block(line[...])

    return pl.pallas_call(
        kern,
        out_shape=(block_of(codes), pltpu.VMEM((codes, width), BF)),
        in_specs=[SCALARS, ANYWHERE, ANYWHERE],
        out_specs=(WHOLE, WHOLE),
        scratch_shapes=[
            pltpu.VMEM((rows, width), BF),
            pltpu.VMEM((1, codes), F32),
            pltpu.VMEM((2, rows, bc), F32),
            pltpu.SemaphoreType.DMA((tiles + 1,)),
        ],
        compiler_params=params(16),
        name="columns_first",
    )(
        me,
        pltpu.with_memory_space_constraint(feats, pltpu.HBM),
        pltpu.with_memory_space_constraint(codebook, pltpu.HBM),
    )


def columns(own, theirs, half, lse_own, bc=256):
    rows, width = own.shape
    codes = half.shape[0]

    def kern(own_ref, f_ref, c_ref, first_ref, o_ref, t_ref, lse_ref, buf):
        t_ref[:, :rows] = own_ref[...].T
        t_ref[:, rows:] = f_ref[...].T
        columns_body(f_ref, c_ref, lse_ref, buf, bc)
        lse = lse_of([first_ref[...], to_block(lse_ref[...])])
        o_ref[...] = jnp.broadcast_to(lse[None], o_ref.shape)

    return pl.pallas_call(
        kern,
        out_shape=(copies_of(16, codes), pltpu.VMEM((width, 2 * rows), BF)),
        in_specs=[WHOLE] * 4,
        out_specs=(WHOLE, WHOLE),
        scratch_shapes=[pltpu.VMEM((1, codes), F32), pltpu.VMEM((2, rows, bc), F32)],
        compiler_params=params(12),
        name="columns",
    )(own, theirs, held(half), lse_own)


def rows_first(me, own, theirs, half, lses, target, rb=256, cb=512):
    rows = 2 * own.shape[0]
    codes = half.shape[0]
    blocks, tiles = rows // rb, codes // cb
    per = rb // tiles

    def kern(me_ref, own_ref, their_ref, c_ref, l_ref, a_ref, lse_ref, peak_ref, out_ref, buf, kept, line, peak_line, col_ref):
        out_ref[...] = target - lse_of([l_ref[k] for k in range(16)])
        col_ref[...] = to_line(out_ref[...])

        def product(b, j):
            f_ref = own_ref if b < blocks // 2 else their_ref
            at = b % (blocks // 2) * rb
            buf[b % 2, :, j * cb : (j + 1) * cb] = lax.dot_general(
                f_ref[at : at + rb, :], c_ref[j * cb : (j + 1) * cb, :], NT, preferred_element_type=F32
            )

        def scale(b, j):
            at = pl.ds(j * per, per)
            val = buf[b % 2, at, :] + col_ref[...]
            peak = jnp.max(val, axis=1, keepdims=True)
            ex = jnp.exp(val - peak)
            total = jnp.sum(ex, axis=1, keepdims=True)
            a_ref[b * rb + j * per : b * rb + (j + 1) * per, :] = ex.astype(BF)
            kept[at, 0:1] = peak
            kept[at, 1:2] = peak + jnp.log(total)

        for j in range(tiles):
            product(0, j)
        for b in range(blocks):
            for j in range(tiles):
                if b + 1 < blocks:
                    product(b + 1, j)
                scale(b, j)
            at = slice(b * rb, (b + 1) * rb)
            peak_line[:, at] = to_row(kept[:, 0:1])
            line[:, at] = to_row(kept[:, 1:2])
        peak_ref[...] = to_block(peak_line[...])
        lse_ref[...] = jnp.broadcast_to(swapped(me_ref, to_block(line[...]))[None], lse_ref.shape)

    return pl.pallas_call(
        kern,
        out_shape=(
            pltpu.VMEM((rows, codes), BF),
            copies_of(8, rows),
            block_of(rows),
            block_of(codes),
        ),
        in_specs=[SCALARS] + [WHOLE] * 4,
        out_specs=(WHOLE,) * 4,
        scratch_shapes=[
            pltpu.VMEM((2, rb, codes), F32),
            pltpu.VMEM((rb, 128), F32),
            pltpu.VMEM((1, rows), F32),
            pltpu.VMEM((1, rows), F32),
            pltpu.VMEM((1, codes), F32),
        ],
        compiler_params=params(20),
        name="rows_first",
    )(me, own, theirs, held(half), lses)


def add_rows(lhs, a_ref, s_ref, line, nb=512):
    for j in range(a_ref.shape[1] // nb):
        at = slice(j * nb, (j + 1) * nb)
        out = lax.dot_general(lhs[...], a_ref[:, at], NN, preferred_element_type=F32)
        line[:, at] = jnp.sum(out, axis=0, keepdims=True)
    s_ref[...] = jnp.broadcast_to(to_block(line[...])[None], s_ref.shape)


def col_sums_first(me, scaled, lses, peak):
    rows, codes = scaled.shape

    def kern(me_ref, a_ref, l_ref, p_ref, s_ref, r_ref, w_ref, lhs, line):
        pot = swapped(me_ref, -lse_of([l_ref[k] for k in range(8)]))
        weight = jnp.exp(p_ref[...] + pot)
        r_ref[...] = pot
        w_ref[...] = weight
        lhs[...] = split_rows(to_line(weight))
        add_rows(lhs, a_ref, s_ref, line)

    return pl.pallas_call(
        kern,
        out_shape=(
            copies_of(16, codes),
            block_of(rows),
            block_of(rows),
        ),
        in_specs=[SCALARS] + [WHOLE] * 3,
        out_specs=(WHOLE,) * 3,
        scratch_shapes=[pltpu.VMEM((16, rows), BF), pltpu.VMEM((1, codes), F32)],
        compiler_params=params(12),
        name="col_sums_first",
    )(me, held(scaled), lses, peak)


def col_sums(me, scaled, totals, weight):
    rows, codes = scaled.shape

    def kern(me_ref, a_ref, t_ref, w_ref, s_ref, lhs, line):
        lhs[...] = split_rows(to_line(w_ref[...] / swapped(me_ref, sum(t_ref[k] for k in range(8)))))
        add_rows(lhs, a_ref, s_ref, line)

    return pl.pallas_call(
        kern,
        out_shape=copies_of(16, codes),
        in_specs=[SCALARS] + [WHOLE] * 3,
        out_specs=WHOLE,
        scratch_shapes=[pltpu.VMEM((16, rows), BF), pltpu.VMEM((1, codes), F32)],
        compiler_params=params(12),
        name="col_sums",
    )(me, held(scaled), totals, weight)


def row_sums(me, scaled, weight, sums, first_col, scale, rb=512):
    rows, codes = scaled.shape

    def kern(me_ref, a_ref, w_ref, s_ref, c_ref, t_ref, col_ref, lhs, line):
        ratio = scale / sum(s_ref[k] for k in range(16))
        col_ref[...] = c_ref[...] + jnp.log(ratio)
        lhs[...] = split_rows(to_line(ratio))
        for j in range(rows // rb):
            at = slice(j * rb, (j + 1) * rb)
            out = lax.dot_general(lhs[...], a_ref[at, :], NT, preferred_element_type=F32)
            line[:, at] = jnp.sum(out, axis=0, keepdims=True)
        total = to_block(line[...]) * w_ref[...]
        t_ref[...] = jnp.broadcast_to(swapped(me_ref, total)[None], t_ref.shape)

    return pl.pallas_call(
        kern,
        out_shape=(copies_of(8, rows), block_of(codes)),
        in_specs=[SCALARS] + [WHOLE] * 4,
        out_specs=(WHOLE, WHOLE),
        scratch_shapes=[pltpu.VMEM((16, codes), BF), pltpu.VMEM((1, rows), F32)],
        compiler_params=params(12),
        name="row_sums",
    )(me, held(scaled), weight, sums, first_col)


def weigh(me, feats_t, totals, weight, first_row):
    width, rows = feats_t.shape

    def kern(me_ref, f_ref, t_ref, w_ref, r_ref, lhs_ref, row_ref):
        total = swapped(me_ref, sum(t_ref[k] for k in range(8)))
        rho = to_line(w_ref[...] / total)
        row_ref[...] = (r_ref[...] - jnp.log(total))[: rows // 256]
        lhs_ref[pl.ds(0, width), :] = (f_ref[...].astype(F32) * rho).astype(BF)
        lhs_ref[pl.ds(width, 16), :] = split_rows(rho)

    return pl.pallas_call(
        kern,
        out_shape=(pltpu.VMEM((width + 16, rows), BF), block_of(rows // 2)),
        in_specs=[SCALARS] + [WHOLE] * 4,
        out_specs=(WHOLE, WHOLE),
        compiler_params=params(16),
        name="weigh",
    )(me, held(feats_t), totals, weight, first_row)


def mass_rows(mass):
    hi = mass.astype(BF).astype(F32)
    row = lax.broadcasted_iota(jnp.int32, (16, mass.shape[1]), 0)
    return jnp.where(row == 0, hi, jnp.where(row == 1, mass - hi, 0.0))


def numerators(me, distance, lhs, scaled, dtype, lanes):
    height = lhs.shape[0]
    width = height - 16

    def kern(me_ref, l_ref, a_ref, o_ref):
        chunk = (coordinates(me_ref)[1] + distance) & 3
        for q in range(scaled.shape[1] // lanes):

            @pl.when(chunk == q)
            def _():
                at = slice(q * lanes, (q + 1) * lanes)
                out = lax.dot_general(l_ref[...], a_ref[:, at], NN, preferred_element_type=F32)
                mass = jnp.sum(out[width:], axis=0, keepdims=True)
                o_ref[pl.ds(0, width), :] = out[:width].astype(dtype)
                o_ref[pl.ds(width, 16), :] = mass_rows(mass).astype(dtype)

    return pl.pallas_call(
        kern,
        out_shape=jax.ShapeDtypeStruct((height, lanes), dtype),
        in_specs=[SCALARS, WHOLE, WHOLE],
        out_specs=WHOLE,
        compiler_params=params(12),
        cost_estimate=cost(1000),
        name="numerators",
    )(me, held(lhs), held(scaled))


def add_first(me, own, arrived):
    height, lanes = own.shape
    width = height - 16
    piece = lanes // 4

    def kern(me_ref, own_ref, r1, r2, r3, *outs):
        for d in range(4):
            at = pl.ds(pl.multiple_of(((coordinates(me_ref)[2] + d) & 3) * piece, piece), piece)
            total = own_ref[:, at]
            for r in (r1, r2, r3):
                total = total + r[:, at].astype(F32)
            mass = jnp.sum(total[width:], axis=0, keepdims=True)
            outs[d][pl.ds(0, width), :] = total[:width].astype(outs[d].dtype)
            outs[d][pl.ds(width, 16), :] = mass_rows(mass).astype(outs[d].dtype)

    return pl.pallas_call(
        kern,
        out_shape=[jax.ShapeDtypeStruct((height, piece), F32 if d == 0 else BF) for d in range(4)],
        in_specs=[SCALARS] + [WHOLE] * 4,
        out_specs=[WHOLE] * 4,
        compiler_params=params(12),
        name="add_first",
    )(me, own, *arrived)


def add_second(own, arrived):
    height, lanes = own.shape
    width = height - 16

    def kern(own_ref, r1, r2, r3, o_ref):
        total = own_ref[...]
        for r in (r1, r2, r3):
            total = total + r[...].astype(F32)
        mass = jnp.sum(total[width:], axis=0, keepdims=True)
        o_ref[...] = (total[:width] / mass).T.astype(BF)

    return pl.pallas_call(
        kern,
        out_shape=jax.ShapeDtypeStruct((lanes, width), BF),
        in_specs=[WHOLE] * 4,
        out_specs=WHOLE,
        compiler_params=params(12),
        name="add_second",
    )(own, *arrived)


def pair(upper, lower):
    rows, width = upper.shape

    def kern(u_ref, l_ref, o_ref):
        o_ref[:rows, :] = u_ref[...]
        o_ref[rows:, :] = l_ref[...]

    return pl.pallas_call(
        kern,
        out_shape=jax.ShapeDtypeStruct((2 * rows, width), upper.dtype),
        in_specs=[WHOLE] * 2,
        out_specs=WHOLE,
        compiler_params=params(8),
        name="pair",
    )(upper, lower)


def assemble(base, shape, pairs, me):
    count = len(pairs)
    rows = pairs[0][0].shape[0] // 2

    def kern(me_ref, *refs):
        core, first, second = coordinates(me_ref)
        o_ref, sems = refs[-2], refs[-1]
        copies = []
        for i, (_, other, back, halves) in enumerate(pairs):
            a, b, c = (1 - core, second, first) if other else (core, first, second)
            for h in range(2):
                index = a * 16 + ((b - back) & 3) * 4 + ((c - halves[h]) & 3)
                at = pl.ds(pl.multiple_of(index * rows, rows), rows)
                copies.append(
                    pltpu.make_async_copy(refs[i].at[pl.ds(h * rows, rows), :], o_ref.at[at, :], sems.at[2 * i + h])
                )
        for c in copies:
            c.start()
        for c in copies:
            c.wait()

    given = [] if base is None else [base]
    return pl.pallas_call(
        kern,
        out_shape=jax.ShapeDtypeStruct(shape, pairs[0][0].dtype),
        in_specs=[SCALARS] + [WHOLE] * count + [ANYWHERE] * len(given),
        out_specs=ANYWHERE,
        scratch_shapes=[pltpu.SemaphoreType.DMA((2 * count,))],
        input_output_aliases={} if base is None else {1 + count: 0},
        compiler_params=params(8),
        name="assemble",
    )(me, *[held(p) for p, _, _, _ in pairs], *given)


def per_device(features, codebook):
    me = lax.axis_index("pts").astype(jnp.int32).reshape(1)
    codes = codebook.shape[0] // 2
    total_rows = features.shape[0] * lax.axis_size("pts")
    total_codes = codebook.shape[0] * lax.axis_size("code")
    target = math.log(total_rows / total_codes)

    theirs = other_core(features)
    lse_own, half = columns_first(me, features, codebook, codes)
    lse, feats_t = columns(features, theirs, half, lse_own)

    def over_chips(value):
        group = [[place(a, b, c) for a in range(4) for b in range(4)] for c in range(2)]
        return lax.all_to_all(value, "pts", 0, 0, tiled=True, axis_index_groups=group)

    def across(value):
        group = [
            [place(a, b, c) * 4 + z for c in range(2) for z in range(4)]
            for a in range(4) for b in range(4)
        ]
        return lax.all_to_all(value, ("pts", "code"), 0, 0, tiled=True, axis_index_groups=group)

    scale = math.exp(target)
    scaled, lses, peak, first_col = rows_first(me, features, theirs, half, over_chips(lse), target)
    sums, first_row, weight = col_sums_first(me, scaled, across(lses), peak)
    totals, _ = row_sums(me, scaled, weight, over_chips(sums), first_col, scale)
    sums = col_sums(me, scaled, across(totals), weight)
    totals, col_pot = row_sums(me, scaled, weight, over_chips(sums), first_col, scale)
    totals, col_pot, feats_t = lax.optimization_barrier((across(totals), col_pot, feats_t))
    lhs, row_pot = weigh(me, feats_t, totals, weight, first_row)

    arrived = []
    for d in (3, 1, 2):
        arrived.append(first_axis(numerators(me, d, lhs, scaled, BF, codes // 4), d))
    own = numerators(me, 0, lhs, scaled, F32, codes // 4)
    pieces = add_first(me, own, arrived)
    arrived = [second_axis(pieces[d], d) for d in (2, 1, 3)]
    fresh = add_second(pieces[0], arrived)

    my_rows = row_pot.reshape(-1)
    their_col = other_core(col_pot)
    cols = jnp.where(me[0] & 1 == 0, jnp.stack([col_pot, their_col]), jnp.stack([their_col, col_pot])).reshape(-1)
    fresh, my_rows, cols = lax.optimization_barrier((fresh, my_rows, cols))

    one, three, two = lax.optimization_barrier(tuple(second_axis(fresh, d) for d in (1, 3, 2)))
    near, far = pair(fresh, one), pair(three, two)

    def placed(value, back, kind):
        halves = (0, 1) if kind == 0 else (3, 2)
        return [
            (value, False, back, halves),
            (other_core(value), True, back, halves),
        ]

    near_1, far_3 = first_axis(near, 1), first_axis(far, 3)
    far_1, near_3 = first_axis(far, 1), first_axis(near, 3)
    near_2, far_2 = first_axis(near_1, 1), first_axis(far_3, 3)
    out = assemble(None, codebook.shape, placed(near, 0, 0) + placed(far, 0, 1), me)
    near_2, out = lax.optimization_barrier((near_2, out))
    out = assemble(out, codebook.shape, placed(near_1, 1, 0) + placed(far_3, 3, 1), me)
    rest = placed(far_1, 1, 1) + placed(near_3, 3, 0) + placed(near_2, 2, 0) + placed(far_2, 2, 1)
    out = assemble(out, codebook.shape, rest, me)
    return out, my_rows, cols


def solution(mesh):
    return jax.shard_map(
        per_device,
        mesh=mesh,
        in_specs=(P("pts", None), P("code", None)),
        out_specs=(P("code", None), P("pts"), P("code")),
        check_vma=False,
    )
```

```python
import functools
import math

import jax
import jax.numpy as jnp
from jax import lax
from jax.experimental import pallas as pl
from jax.experimental.pallas import tpu as pltpu
from jax.sharding import PartitionSpec as P

BF = jnp.bfloat16
F32 = jnp.float32
NT = (((1,), (1,)), ((), ()))
NN = (((1,), (0,)), ((), ()))


def place(x, y, c):
    return ((x % 4) * 4 + (y % 4)) * 2 + c


def shift(value, move):
    pairs = []
    for x in range(4):
        for y in range(4):
            for c in range(2):
                pairs.append((place(x, y, c), place(*move(x, y, c))))
    return lax.ppermute(value, "pts", pairs)


def other_core(value):
    return shift(value, lambda x, y, c: (x, y, 1 - c))


def first_axis(value, d):
    return shift(value, lambda x, y, c: (x + d * c, y + d * (1 - c), c))


def second_axis(value, d):
    return shift(value, lambda x, y, c: (x + d * (1 - c), y + d * c, c))


def params(mib=32):
    return pltpu.CompilerParams(vmem_limit_bytes=mib * 1024 * 1024)


def cost(flops):
    return pl.CostEstimate(flops=flops, bytes_accessed=0, transcendentals=0)


def held(value):
    return pltpu.with_memory_space_constraint(value, pltpu.VMEM)


def lse_of(parts):
    peak = functools.reduce(jnp.maximum, parts)
    return peak + jnp.log(sum(jnp.exp(p - peak) for p in parts))


def split_rows(v):
    n = v.shape[1]
    hi = v.astype(BF).astype(F32)
    mid = (v - hi).astype(BF).astype(F32)
    low = v - hi - mid
    row = lax.broadcasted_iota(jnp.int32, (16, n), 0)
    return jnp.where(row == 0, hi, jnp.where(row == 1, mid, jnp.where(row == 2, low, 0.0))).astype(BF)


def coordinates(me_ref):
    me = me_ref[0]
    core, y, x = me & 1, (me >> 1) & 3, me >> 3
    return core, jnp.where(core == 0, y, x), jnp.where(core == 0, x, y)


def to_block(line):
    return jnp.concatenate([line[:, i : i + 128] for i in range(0, line.shape[1], 128)], axis=0)


def to_line(block):
    return jnp.concatenate([block[i : i + 1] for i in range(block.shape[0])], axis=1)


def swapped(me_ref, block):
    n = block.shape[0] // 2
    return jnp.where(coordinates(me_ref)[0] == 0, block, jnp.concatenate([block[n:], block[:n]], axis=0))


def copies_of(count, n):
    return jax.ShapeDtypeStruct((count, n // 128, 128), F32)


def block_of(n):
    return jax.ShapeDtypeStruct((n // 128, 128), F32)


def to_row(col):
    n = col.shape[0]
    diag = lax.broadcasted_iota(jnp.int32, (128, 128), 0) == lax.broadcasted_iota(jnp.int32, (128, 128), 1)
    parts = []
    for i in range(0, n, 128):
        parts.append(jnp.sum(jnp.where(diag, col[i : i + 128], 0.0), axis=0, keepdims=True))
    return jnp.concatenate(parts, axis=1)


WHOLE = pl.BlockSpec(memory_space=pltpu.VMEM)
SCALARS = pl.BlockSpec(memory_space=pltpu.SMEM)
ANYWHERE = pl.BlockSpec(memory_space=pl.ANY)


def columns_body(f_ref, c_ref, o_ref, buf, bc, first=0, last=None):
    last = c_ref.shape[0] // bc if last is None else last

    def product(j):
        buf[j % 2] = lax.dot_general(
            f_ref[...], c_ref[j * bc : (j + 1) * bc, :], NT, preferred_element_type=F32
        )

    product(first)
    for j in range(first, last):
        if j + 1 < last:
            product(j + 1)
        part = buf.at[j % 2]
        peak = jnp.max(part[...], axis=0, keepdims=True)
        total = jnp.sum(jnp.exp(part[...] - peak), axis=0, keepdims=True)
        o_ref[:, j * bc : (j + 1) * bc] = peak + jnp.log(total)


def columns_first(me, feats, codebook, codes, bc=256):
    rows, width = feats.shape
    tiles = codes // bc

    def kern(me_ref, f_hbm, c_hbm, o_ref, half_ref, f_ref, line, buf, sems):
        copies = [pltpu.make_async_copy(f_hbm, f_ref, sems.at[tiles])]
        for j in range(tiles):
            start = pl.multiple_of(coordinates(me_ref)[0] * codes + j * bc, bc)
            copies.append(
                pltpu.make_async_copy(
                    c_hbm.at[pl.ds(start, bc), :], half_ref.at[pl.ds(j * bc, bc), :], sems.at[j]
                )
            )
        for c in copies:
            c.start()
        middle = tiles // 4
        for c in copies[: 1 + middle]:
            c.wait()
        columns_body(f_ref, half_ref, line, buf, bc, 0, middle)
        for c in copies[1 + middle :]:
            c.wait()
        columns_body(f_ref, half_ref, line, buf, bc, middle, tiles)
        o_ref[...] = to_block(line[...])

    return pl.pallas_call(
        kern,
        out_shape=(block_of(codes), pltpu.VMEM((codes, width), BF)),
        in_specs=[SCALARS, ANYWHERE, ANYWHERE],
        out_specs=(WHOLE, WHOLE),
        scratch_shapes=[
            pltpu.VMEM((rows, width), BF),
            pltpu.VMEM((1, codes), F32),
            pltpu.VMEM((2, rows, bc), F32),
            pltpu.SemaphoreType.DMA((tiles + 1,)),
        ],
        compiler_params=params(16),
        name="columns_first",
    )(
        me,
        pltpu.with_memory_space_constraint(feats, pltpu.HBM),
        pltpu.with_memory_space_constraint(codebook, pltpu.HBM),
    )


def columns(own, theirs, half, lse_own, bc=256):
    rows, width = own.shape
    codes = half.shape[0]

    def kern(own_ref, f_ref, c_ref, first_ref, o_ref, t_ref, lse_ref, buf):
        t_ref[:, :rows] = own_ref[...].T
        t_ref[:, rows:] = f_ref[...].T
        columns_body(f_ref, c_ref, lse_ref, buf, bc)
        lse = lse_of([first_ref[...], to_block(lse_ref[...])])
        o_ref[...] = jnp.broadcast_to(lse[None], o_ref.shape)

    return pl.pallas_call(
        kern,
        out_shape=(copies_of(16, codes), pltpu.VMEM((width, 2 * rows), BF)),
        in_specs=[WHOLE] * 4,
        out_specs=(WHOLE, WHOLE),
        scratch_shapes=[pltpu.VMEM((1, codes), F32), pltpu.VMEM((2, rows, bc), F32)],
        compiler_params=params(12),
        name="columns",
    )(own, theirs, held(half), lse_own)


def rows_first(me, own, theirs, half, lses, target, rb=256, cb=512):
    rows = 2 * own.shape[0]
    codes = half.shape[0]
    blocks, tiles = rows // rb, codes // cb
    per = rb // tiles

    def kern(me_ref, own_ref, their_ref, c_ref, l_ref, a_ref, lse_ref, peak_ref, out_ref, buf, kept, line, peak_line, col_ref):
        out_ref[...] = target - lse_of([l_ref[k] for k in range(16)])
        col_ref[...] = to_line(out_ref[...])

        def product(b, j):
            f_ref = own_ref if b < blocks // 2 else their_ref
            at = b % (blocks // 2) * rb
            buf[b % 2, :, j * cb : (j + 1) * cb] = lax.dot_general(
                f_ref[at : at + rb, :], c_ref[j * cb : (j + 1) * cb, :], NT, preferred_element_type=F32
            )

        def scale(b, j):
            at = pl.ds(j * per, per)
            val = buf[b % 2, at, :] + col_ref[...]
            peak = jnp.max(val, axis=1, keepdims=True)
            ex = jnp.exp(val - peak)
            total = jnp.sum(ex, axis=1, keepdims=True)
            a_ref[b * rb + j * per : b * rb + (j + 1) * per, :] = ex.astype(BF)
            kept[at, 0:1] = peak
            kept[at, 1:2] = peak + jnp.log(total)

        for j in range(tiles):
            product(0, j)
        for b in range(blocks):
            for j in range(tiles):
                if b + 1 < blocks:
                    product(b + 1, j)
                scale(b, j)
            at = slice(b * rb, (b + 1) * rb)
            peak_line[:, at] = to_row(kept[:, 0:1])
            line[:, at] = to_row(kept[:, 1:2])
        peak_ref[...] = to_block(peak_line[...])
        lse_ref[...] = jnp.broadcast_to(swapped(me_ref, to_block(line[...]))[None], lse_ref.shape)

    return pl.pallas_call(
        kern,
        out_shape=(
            pltpu.VMEM((rows, codes), BF),
            copies_of(8, rows),
            block_of(rows),
            block_of(codes),
        ),
        in_specs=[SCALARS] + [WHOLE] * 4,
        out_specs=(WHOLE,) * 4,
        scratch_shapes=[
            pltpu.VMEM((2, rb, codes), F32),
            pltpu.VMEM((rb, 128), F32),
            pltpu.VMEM((1, rows), F32),
            pltpu.VMEM((1, rows), F32),
            pltpu.VMEM((1, codes), F32),
        ],
        compiler_params=params(20),
        name="rows_first",
    )(me, own, theirs, held(half), lses)


def add_rows(lhs, a_ref, s_ref, line, nb=512):
    for j in range(a_ref.shape[1] // nb):
        at = slice(j * nb, (j + 1) * nb)
        out = lax.dot_general(lhs[...], a_ref[:, at], NN, preferred_element_type=F32)
        line[:, at] = jnp.sum(out, axis=0, keepdims=True)
    s_ref[...] = jnp.broadcast_to(to_block(line[...])[None], s_ref.shape)


def col_sums_first(me, scaled, lses, peak):
    rows, codes = scaled.shape

    def kern(me_ref, a_ref, l_ref, p_ref, s_ref, r_ref, w_ref, lhs, line):
        pot = swapped(me_ref, -lse_of([l_ref[k] for k in range(8)]))
        weight = jnp.exp(p_ref[...] + pot)
        r_ref[...] = pot
        w_ref[...] = weight
        lhs[...] = split_rows(to_line(weight))
        add_rows(lhs, a_ref, s_ref, line)

    return pl.pallas_call(
        kern,
        out_shape=(
            copies_of(16, codes),
            block_of(rows),
            block_of(rows),
        ),
        in_specs=[SCALARS] + [WHOLE] * 3,
        out_specs=(WHOLE,) * 3,
        scratch_shapes=[pltpu.VMEM((16, rows), BF), pltpu.VMEM((1, codes), F32)],
        compiler_params=params(12),
        name="col_sums_first",
    )(me, held(scaled), lses, peak)


def col_sums(me, scaled, totals, weight):
    rows, codes = scaled.shape

    def kern(me_ref, a_ref, t_ref, w_ref, s_ref, lhs, line):
        lhs[...] = split_rows(to_line(w_ref[...] / swapped(me_ref, sum(t_ref[k] for k in range(8)))))
        add_rows(lhs, a_ref, s_ref, line)

    return pl.pallas_call(
        kern,
        out_shape=copies_of(16, codes),
        in_specs=[SCALARS] + [WHOLE] * 3,
        out_specs=WHOLE,
        scratch_shapes=[pltpu.VMEM((16, rows), BF), pltpu.VMEM((1, codes), F32)],
        compiler_params=params(12),
        name="col_sums",
    )(me, held(scaled), totals, weight)


def row_sums(me, scaled, weight, sums, first_col, scale, rb=256, rest=1024):
    rows, codes = scaled.shape
    share = rest * rb // (rows - rest)

    def kern(me_ref, a_ref, w_ref, s_ref, c_ref, t_ref, col_ref, lhs, line):
        ratio = scale / sum(s_ref[k] for k in range(16))
        col_ref[...] = c_ref[...] + jnp.log(ratio)
        lhs[...] = split_rows(to_line(ratio))
        ratios = to_line(ratio)
        split = rows - rest
        for j in range(split // rb):
            at = slice(j * rb, (j + 1) * rb)
            out = lax.dot_general(lhs[...], a_ref[at, :], NT, preferred_element_type=F32)
            line[:, at] = jnp.sum(out, axis=0, keepdims=True)
            for r in range(split + j * share, split + (j + 1) * share, 128):
                acc = jnp.zeros((128, 128), F32)
                for k in range(0, codes, 128):
                    acc = acc + a_ref[r : r + 128, k : k + 128].astype(F32) * ratios[:, k : k + 128]
                line[:, r : r + 128] = to_row(jnp.sum(acc, axis=1, keepdims=True))
        total = to_block(line[...]) * w_ref[...]
        t_ref[...] = jnp.broadcast_to(swapped(me_ref, total)[None], t_ref.shape)

    return pl.pallas_call(
        kern,
        out_shape=(copies_of(8, rows), block_of(codes)),
        in_specs=[SCALARS] + [WHOLE] * 4,
        out_specs=(WHOLE, WHOLE),
        scratch_shapes=[pltpu.VMEM((16, codes), BF), pltpu.VMEM((1, rows), F32)],
        compiler_params=params(12),
        name="row_sums",
    )(me, held(scaled), weight, sums, first_col)


def weigh(me, feats_t, totals, weight, first_row):
    width, rows = feats_t.shape

    def kern(me_ref, f_ref, t_ref, w_ref, r_ref, lhs_ref, row_ref):
        total = swapped(me_ref, sum(t_ref[k] for k in range(8)))
        rho = to_line(w_ref[...] / total)
        row_ref[...] = (r_ref[...] - jnp.log(total))[: rows // 256]
        lhs_ref[pl.ds(0, width), :] = (f_ref[...].astype(F32) * rho).astype(BF)
        lhs_ref[pl.ds(width, 16), :] = split_rows(rho)

    return pl.pallas_call(
        kern,
        out_shape=(pltpu.VMEM((width + 16, rows), BF), block_of(rows // 2)),
        in_specs=[SCALARS] + [WHOLE] * 4,
        out_specs=(WHOLE, WHOLE),
        compiler_params=params(16),
        name="weigh",
    )(me, held(feats_t), totals, weight, first_row)


def mass_rows(mass):
    hi = mass.astype(BF).astype(F32)
    row = lax.broadcasted_iota(jnp.int32, (16, mass.shape[1]), 0)
    return jnp.where(row == 0, hi, jnp.where(row == 1, mass - hi, 0.0))


def numerators(me, distance, lhs, scaled, dtype, lanes):
    height = lhs.shape[0]
    width = height - 16

    def kern(me_ref, l_ref, a_ref, o_ref):
        chunk = (coordinates(me_ref)[1] + distance) & 3
        for q in range(scaled.shape[1] // lanes):

            @pl.when(chunk == q)
            def _():
                at = slice(q * lanes, (q + 1) * lanes)
                out = lax.dot_general(l_ref[...], a_ref[:, at], NN, preferred_element_type=F32)
                mass = jnp.sum(out[width:], axis=0, keepdims=True)
                o_ref[pl.ds(0, width), :] = out[:width].astype(dtype)
                o_ref[pl.ds(width, 16), :] = mass_rows(mass).astype(dtype)

    return pl.pallas_call(
        kern,
        out_shape=jax.ShapeDtypeStruct((height, lanes), dtype),
        in_specs=[SCALARS, WHOLE, WHOLE],
        out_specs=WHOLE,
        compiler_params=params(12),
        cost_estimate=cost(1000),
        name="numerators",
    )(me, held(lhs), held(scaled))


def add_first(me, own, arrived):
    height, lanes = own.shape
    width = height - 16
    piece = lanes // 4

    def kern(me_ref, own_ref, r1, r2, r3, *outs):
        for d in range(4):
            at = pl.ds(pl.multiple_of(((coordinates(me_ref)[2] + d) & 3) * piece, piece), piece)
            total = own_ref[:, at]
            for r in (r1, r2, r3):
                total = total + r[:, at].astype(F32)
            mass = jnp.sum(total[width:], axis=0, keepdims=True)
            outs[d][pl.ds(0, width), :] = total[:width].astype(outs[d].dtype)
            outs[d][pl.ds(width, 16), :] = mass_rows(mass).astype(outs[d].dtype)

    return pl.pallas_call(
        kern,
        out_shape=[jax.ShapeDtypeStruct((height, piece), F32 if d == 0 else BF) for d in range(4)],
        in_specs=[SCALARS] + [WHOLE] * 4,
        out_specs=[WHOLE] * 4,
        compiler_params=params(12),
        name="add_first",
    )(me, own, *arrived)


def add_second(own, arrived):
    height, lanes = own.shape
    width = height - 16

    def kern(own_ref, r1, r2, r3, o_ref):
        total = own_ref[...]
        for r in (r1, r2, r3):
            total = total + r[...].astype(F32)
        mass = jnp.sum(total[width:], axis=0, keepdims=True)
        o_ref[...] = (total[:width] / mass).T.astype(BF)

    return pl.pallas_call(
        kern,
        out_shape=jax.ShapeDtypeStruct((lanes, width), BF),
        in_specs=[WHOLE] * 4,
        out_specs=WHOLE,
        compiler_params=params(12),
        name="add_second",
    )(own, *arrived)


def pair(upper, lower):
    rows, width = upper.shape

    def kern(u_ref, l_ref, o_ref):
        o_ref[:rows, :] = u_ref[...]
        o_ref[rows:, :] = l_ref[...]

    return pl.pallas_call(
        kern,
        out_shape=jax.ShapeDtypeStruct((2 * rows, width), upper.dtype),
        in_specs=[WHOLE] * 2,
        out_specs=WHOLE,
        compiler_params=params(8),
        name="pair",
    )(upper, lower)


def assemble(base, shape, pairs, me):
    count = len(pairs)
    rows = pairs[0][0].shape[0] // 2

    def kern(me_ref, *refs):
        core, first, second = coordinates(me_ref)
        o_ref, sems = refs[-2], refs[-1]
        copies = []
        for i, (_, other, back, halves) in enumerate(pairs):
            a, b, c = (1 - core, second, first) if other else (core, first, second)
            for h in range(2):
                index = a * 16 + ((b - back) & 3) * 4 + ((c - halves[h]) & 3)
                at = pl.ds(pl.multiple_of(index * rows, rows), rows)
                copies.append(
                    pltpu.make_async_copy(refs[i].at[pl.ds(h * rows, rows), :], o_ref.at[at, :], sems.at[2 * i + h])
                )
        for c in copies:
            c.start()
        for c in copies:
            c.wait()

    given = [] if base is None else [base]
    return pl.pallas_call(
        kern,
        out_shape=jax.ShapeDtypeStruct(shape, pairs[0][0].dtype),
        in_specs=[SCALARS] + [WHOLE] * count + [ANYWHERE] * len(given),
        out_specs=ANYWHERE,
        scratch_shapes=[pltpu.SemaphoreType.DMA((2 * count,))],
        input_output_aliases={} if base is None else {1 + count: 0},
        compiler_params=params(8),
        name="assemble",
    )(me, *[held(p) for p, _, _, _ in pairs], *given)


def per_device(features, codebook):
    me = lax.axis_index("pts").astype(jnp.int32).reshape(1)
    codes = codebook.shape[0] // 2
    total_rows = features.shape[0] * lax.axis_size("pts")
    total_codes = codebook.shape[0] * lax.axis_size("code")
    target = math.log(total_rows / total_codes)

    theirs = other_core(features)
    lse_own, half = columns_first(me, features, codebook, codes)
    lse, feats_t = columns(features, theirs, half, lse_own)

    def over_chips(value):
        group = [[place(a, b, c) for a in range(4) for b in range(4)] for c in range(2)]
        return lax.all_to_all(value, "pts", 0, 0, tiled=True, axis_index_groups=group)

    def across(value):
        group = [
            [place(a, b, c) * 4 + z for c in range(2) for z in range(4)]
            for a in range(4) for b in range(4)
        ]
        return lax.all_to_all(value, ("pts", "code"), 0, 0, tiled=True, axis_index_groups=group)

    scale = math.exp(target)
    scaled, lses, peak, first_col = rows_first(me, features, theirs, half, over_chips(lse), target)
    sums, first_row, weight = col_sums_first(me, scaled, across(lses), peak)
    totals, _ = row_sums(me, scaled, weight, over_chips(sums), first_col, scale)
    sums = col_sums(me, scaled, across(totals), weight)
    totals, col_pot = row_sums(me, scaled, weight, over_chips(sums), first_col, scale)
    totals, col_pot, feats_t = lax.optimization_barrier((across(totals), col_pot, feats_t))
    lhs, row_pot = weigh(me, feats_t, totals, weight, first_row)

    arrived = []
    for d in (3, 1, 2):
        arrived.append(first_axis(numerators(me, d, lhs, scaled, BF, codes // 4), d))
    own = numerators(me, 0, lhs, scaled, F32, codes // 4)
    pieces = add_first(me, own, arrived)
    arrived = [second_axis(pieces[d], d) for d in (2, 1, 3)]
    fresh = add_second(pieces[0], arrived)

    my_rows = row_pot.reshape(-1)
    their_col = other_core(col_pot)
    cols = jnp.where(me[0] & 1 == 0, jnp.stack([col_pot, their_col]), jnp.stack([their_col, col_pot])).reshape(-1)
    fresh, my_rows, cols = lax.optimization_barrier((fresh, my_rows, cols))

    one, three, two = lax.optimization_barrier(tuple(second_axis(fresh, d) for d in (1, 3, 2)))
    near, far = pair(fresh, one), pair(three, two)

    def placed(value, back, kind):
        halves = (0, 1) if kind == 0 else (3, 2)
        return [
            (value, False, back, halves),
            (other_core(value), True, back, halves),
        ]

    near_1, far_3 = first_axis(near, 1), first_axis(far, 3)
    far_1, near_3 = first_axis(far, 1), first_axis(near, 3)
    near_2, far_2 = first_axis(near_1, 1), first_axis(far_3, 3)
    out = assemble(None, codebook.shape, placed(near, 0, 0) + placed(far, 0, 1), me)
    near_2, out = lax.optimization_barrier((near_2, out))
    out = assemble(out, codebook.shape, placed(near_1, 1, 0) + placed(far_3, 3, 1), me)
    rest = placed(far_1, 1, 1) + placed(near_3, 3, 0) + placed(near_2, 2, 0) + placed(far_2, 2, 1)
    out = assemble(out, codebook.shape, rest, me)
    return out, my_rows, cols


def solution(mesh):
    return jax.shard_map(
        per_device,
        mesh=mesh,
        in_specs=(P("pts", None), P("code", None)),
        out_specs=(P("code", None), P("pts"), P("code")),
        check_vma=False,
    )
```

```python
import functools
import math

import jax
import jax.numpy as jnp
from jax import lax
from jax.experimental import pallas as pl
from jax.experimental.pallas import tpu as pltpu
from jax.sharding import PartitionSpec as P

BF = jnp.bfloat16
F32 = jnp.float32
NT = (((1,), (1,)), ((), ()))
NN = (((1,), (0,)), ((), ()))


def place(x, y, c):
    return ((x % 4) * 4 + (y % 4)) * 2 + c


def shift(value, move):
    pairs = []
    for x in range(4):
        for y in range(4):
            for c in range(2):
                pairs.append((place(x, y, c), place(*move(x, y, c))))
    return lax.ppermute(value, "pts", pairs)


def other_core(value):
    return shift(value, lambda x, y, c: (x, y, 1 - c))


def first_axis(value, d):
    return shift(value, lambda x, y, c: (x + d * c, y + d * (1 - c), c))


def second_axis(value, d):
    return shift(value, lambda x, y, c: (x + d * (1 - c), y + d * c, c))


def params(mib=32):
    return pltpu.CompilerParams(vmem_limit_bytes=mib * 1024 * 1024)


def cost(flops):
    return pl.CostEstimate(flops=flops, bytes_accessed=0, transcendentals=0)


def held(value):
    return pltpu.with_memory_space_constraint(value, pltpu.VMEM)


def lse_of(parts):
    peak = functools.reduce(jnp.maximum, parts)
    return peak + jnp.log(sum(jnp.exp(p - peak) for p in parts))


def split_rows(v):
    n = v.shape[1]
    hi = v.astype(BF).astype(F32)
    mid = (v - hi).astype(BF).astype(F32)
    low = v - hi - mid
    row = lax.broadcasted_iota(jnp.int32, (16, n), 0)
    return jnp.where(row == 0, hi, jnp.where(row == 1, mid, jnp.where(row == 2, low, 0.0))).astype(BF)


def coordinates(me_ref):
    me = me_ref[0]
    core, y, x = me & 1, (me >> 1) & 3, me >> 3
    return core, jnp.where(core == 0, y, x), jnp.where(core == 0, x, y)


def to_block(line):
    return jnp.concatenate([line[:, i : i + 128] for i in range(0, line.shape[1], 128)], axis=0)


def to_line(block):
    return jnp.concatenate([block[i : i + 1] for i in range(block.shape[0])], axis=1)


def swapped(me_ref, block):
    n = block.shape[0] // 2
    return jnp.where(coordinates(me_ref)[0] == 0, block, jnp.concatenate([block[n:], block[:n]], axis=0))


def copies_of(count, n):
    return jax.ShapeDtypeStruct((count, n // 128, 128), F32)


def block_of(n):
    return jax.ShapeDtypeStruct((n // 128, 128), F32)


def to_row(col):
    n = col.shape[0]
    diag = lax.broadcasted_iota(jnp.int32, (128, 128), 0) == lax.broadcasted_iota(jnp.int32, (128, 128), 1)
    parts = []
    for i in range(0, n, 128):
        parts.append(jnp.sum(jnp.where(diag, col[i : i + 128], 0.0), axis=0, keepdims=True))
    return jnp.concatenate(parts, axis=1)


WHOLE = pl.BlockSpec(memory_space=pltpu.VMEM)
SCALARS = pl.BlockSpec(memory_space=pltpu.SMEM)
ANYWHERE = pl.BlockSpec(memory_space=pl.ANY)


def columns_body(f_ref, c_ref, o_ref, buf, bc, first=0, last=None):
    last = c_ref.shape[0] // bc if last is None else last

    def product(j):
        buf[j % 2] = lax.dot_general(
            f_ref[...], c_ref[j * bc : (j + 1) * bc, :], NT, preferred_element_type=F32
        )

    product(first)
    for j in range(first, last):
        if j + 1 < last:
            product(j + 1)
        part = buf.at[j % 2]
        peak = jnp.max(part[...], axis=0, keepdims=True)
        total = jnp.sum(jnp.exp(part[...] - peak), axis=0, keepdims=True)
        o_ref[:, j * bc : (j + 1) * bc] = peak + jnp.log(total)


def columns_first(me, feats, codebook, codes, bc=256):
    rows, width = feats.shape
    tiles = codes // bc

    def kern(me_ref, f_hbm, c_hbm, o_ref, half_ref, f_ref, line, buf, sems):
        copies = [pltpu.make_async_copy(f_hbm, f_ref, sems.at[tiles])]
        for j in range(tiles):
            start = pl.multiple_of(coordinates(me_ref)[0] * codes + j * bc, bc)
            copies.append(
                pltpu.make_async_copy(
                    c_hbm.at[pl.ds(start, bc), :], half_ref.at[pl.ds(j * bc, bc), :], sems.at[j]
                )
            )
        for c in copies:
            c.start()
        middle = tiles // 4
        for c in copies[: 1 + middle]:
            c.wait()
        columns_body(f_ref, half_ref, line, buf, bc, 0, middle)
        for c in copies[1 + middle :]:
            c.wait()
        columns_body(f_ref, half_ref, line, buf, bc, middle, tiles)
        o_ref[...] = to_block(line[...])

    return pl.pallas_call(
        kern,
        out_shape=(block_of(codes), pltpu.VMEM((codes, width), BF)),
        in_specs=[SCALARS, ANYWHERE, ANYWHERE],
        out_specs=(WHOLE, WHOLE),
        scratch_shapes=[
            pltpu.VMEM((rows, width), BF),
            pltpu.VMEM((1, codes), F32),
            pltpu.VMEM((2, rows, bc), F32),
            pltpu.SemaphoreType.DMA((tiles + 1,)),
        ],
        compiler_params=params(16),
        name="columns_first",
    )(
        me,
        pltpu.with_memory_space_constraint(feats, pltpu.HBM),
        pltpu.with_memory_space_constraint(codebook, pltpu.HBM),
    )


def columns(own, theirs, half, lse_own, bc=256):
    rows, width = own.shape
    codes = half.shape[0]

    def kern(own_ref, f_ref, c_ref, first_ref, o_ref, t_ref, lse_ref, buf):
        t_ref[:, :rows] = own_ref[...].T
        t_ref[:, rows:] = f_ref[...].T
        columns_body(f_ref, c_ref, lse_ref, buf, bc)
        lse = lse_of([first_ref[...], to_block(lse_ref[...])])
        o_ref[...] = jnp.broadcast_to(lse[None], o_ref.shape)

    return pl.pallas_call(
        kern,
        out_shape=(copies_of(16, codes), pltpu.VMEM((width, 2 * rows), BF)),
        in_specs=[WHOLE] * 4,
        out_specs=(WHOLE, WHOLE),
        scratch_shapes=[pltpu.VMEM((1, codes), F32), pltpu.VMEM((2, rows, bc), F32)],
        compiler_params=params(12),
        name="columns",
    )(own, theirs, held(half), lse_own)


def rows_first(me, own, theirs, half, lses, target, rb=256, cb=512):
    rows = 2 * own.shape[0]
    codes = half.shape[0]
    blocks, tiles = rows // rb, codes // cb
    per = rb // tiles

    def kern(me_ref, own_ref, their_ref, c_ref, l_ref, a_ref, lse_ref, peak_ref, out_ref, buf, kept, line, peak_line, col_ref):
        out_ref[...] = target - lse_of([l_ref[k] for k in range(16)])
        col_ref[...] = to_line(out_ref[...])

        def product(b, j):
            f_ref = own_ref if b < blocks // 2 else their_ref
            at = b % (blocks // 2) * rb
            buf[b % 2, :, j * cb : (j + 1) * cb] = lax.dot_general(
                f_ref[at : at + rb, :], c_ref[j * cb : (j + 1) * cb, :], NT, preferred_element_type=F32
            )

        def scale(b, j):
            at = pl.ds(j * per, per)
            val = buf[b % 2, at, :] + col_ref[...]
            peak = jnp.max(val, axis=1, keepdims=True)
            ex = jnp.exp(val - peak)
            total = jnp.sum(ex, axis=1, keepdims=True)
            a_ref[b * rb + j * per : b * rb + (j + 1) * per, :] = ex.astype(BF)
            kept[at, 0:1] = peak
            kept[at, 1:2] = peak + jnp.log(total)

        for j in range(tiles):
            product(0, j)
        for b in range(blocks):
            for j in range(tiles):
                if b + 1 < blocks:
                    product(b + 1, j)
                scale(b, j)
            at = slice(b * rb, (b + 1) * rb)
            peak_line[:, at] = to_row(kept[:, 0:1])
            line[:, at] = to_row(kept[:, 1:2])
        peak_ref[...] = to_block(peak_line[...])
        lse_ref[...] = jnp.broadcast_to(swapped(me_ref, to_block(line[...]))[None], lse_ref.shape)

    return pl.pallas_call(
        kern,
        out_shape=(
            pltpu.VMEM((rows, codes), BF),
            copies_of(8, rows),
            block_of(rows),
            block_of(codes),
        ),
        in_specs=[SCALARS] + [WHOLE] * 4,
        out_specs=(WHOLE,) * 4,
        scratch_shapes=[
            pltpu.VMEM((2, rb, codes), F32),
            pltpu.VMEM((rb, 128), F32),
            pltpu.VMEM((1, rows), F32),
            pltpu.VMEM((1, rows), F32),
            pltpu.VMEM((1, codes), F32),
        ],
        compiler_params=params(20),
        name="rows_first",
    )(me, own, theirs, held(half), lses)


def add_rows(lhs, a_ref, s_ref, line, nb=512):
    for j in range(a_ref.shape[1] // nb):
        at = slice(j * nb, (j + 1) * nb)
        out = lax.dot_general(lhs[...], a_ref[:, at], NN, preferred_element_type=F32)
        line[:, at] = jnp.sum(out, axis=0, keepdims=True)
    s_ref[...] = jnp.broadcast_to(to_block(line[...])[None], s_ref.shape)


def col_sums_first(me, scaled, lses, peak):
    rows, codes = scaled.shape

    def kern(me_ref, a_ref, l_ref, p_ref, s_ref, r_ref, w_ref, lhs, line):
        pot = swapped(me_ref, -lse_of([l_ref[k] for k in range(8)]))
        weight = jnp.exp(p_ref[...] + pot)
        r_ref[...] = pot
        w_ref[...] = weight
        lhs[...] = split_rows(to_line(weight))
        add_rows(lhs, a_ref, s_ref, line)

    return pl.pallas_call(
        kern,
        out_shape=(
            copies_of(16, codes),
            block_of(rows),
            block_of(rows),
        ),
        in_specs=[SCALARS] + [WHOLE] * 3,
        out_specs=(WHOLE,) * 3,
        scratch_shapes=[pltpu.VMEM((16, rows), BF), pltpu.VMEM((1, codes), F32)],
        compiler_params=params(12),
        name="col_sums_first",
    )(me, held(scaled), lses, peak)


def col_sums(me, scaled, totals, weight):
    rows, codes = scaled.shape

    def kern(me_ref, a_ref, t_ref, w_ref, s_ref, lhs, line):
        lhs[...] = split_rows(to_line(w_ref[...] / swapped(me_ref, sum(t_ref[k] for k in range(8)))))
        add_rows(lhs, a_ref, s_ref, line)

    return pl.pallas_call(
        kern,
        out_shape=copies_of(16, codes),
        in_specs=[SCALARS] + [WHOLE] * 3,
        out_specs=WHOLE,
        scratch_shapes=[pltpu.VMEM((16, rows), BF), pltpu.VMEM((1, codes), F32)],
        compiler_params=params(12),
        name="col_sums",
    )(me, held(scaled), totals, weight)


def row_sums(me, scaled, weight, sums, first_col, scale, rb=256, rest=1024):
    rows, codes = scaled.shape
    share = rest * rb // (rows - rest)

    def kern(me_ref, a_ref, w_ref, s_ref, c_ref, t_ref, col_ref, lhs, line):
        ratio = scale / sum(s_ref[k] for k in range(16))
        col_ref[...] = c_ref[...] + jnp.log(ratio)
        lhs[...] = split_rows(to_line(ratio))
        ratios = to_line(ratio)
        split = rows - rest
        for j in range(split // rb):
            at = slice(j * rb, (j + 1) * rb)
            out = lax.dot_general(lhs[...], a_ref[at, :], NT, preferred_element_type=F32)
            line[:, at] = jnp.sum(out, axis=0, keepdims=True)
            for r in range(split + j * share, split + (j + 1) * share, 128):
                acc = jnp.zeros((128, 128), F32)
                for k in range(0, codes, 128):
                    acc = acc + a_ref[r : r + 128, k : k + 128].astype(F32) * ratios[:, k : k + 128]
                line[:, r : r + 128] = to_row(jnp.sum(acc, axis=1, keepdims=True))
        total = to_block(line[...]) * w_ref[...]
        t_ref[...] = jnp.broadcast_to(swapped(me_ref, total)[None], t_ref.shape)

    return pl.pallas_call(
        kern,
        out_shape=(copies_of(8, rows), block_of(codes)),
        in_specs=[SCALARS] + [WHOLE] * 4,
        out_specs=(WHOLE, WHOLE),
        scratch_shapes=[pltpu.VMEM((16, codes), BF), pltpu.VMEM((1, rows), F32)],
        compiler_params=params(12),
        name="row_sums",
    )(me, held(scaled), weight, sums, first_col)


def weigh(me, feats_t, totals, weight, first_row):
    width, rows = feats_t.shape

    def kern(me_ref, f_ref, t_ref, w_ref, r_ref, lhs_ref, row_ref):
        total = swapped(me_ref, sum(t_ref[k] for k in range(8)))
        rho = to_line(w_ref[...] / total)
        row_ref[...] = (r_ref[...] - jnp.log(total))[: rows // 256]
        lhs_ref[pl.ds(0, width), :] = (f_ref[...].astype(F32) * rho).astype(BF)
        lhs_ref[pl.ds(width, 16), :] = split_rows(rho)

    return pl.pallas_call(
        kern,
        out_shape=(pltpu.VMEM((width + 16, rows), BF), block_of(rows // 2)),
        in_specs=[SCALARS] + [WHOLE] * 4,
        out_specs=(WHOLE, WHOLE),
        compiler_params=params(16),
        name="weigh",
    )(me, held(feats_t), totals, weight, first_row)


def mass_rows(mass):
    hi = mass.astype(BF).astype(F32)
    row = lax.broadcasted_iota(jnp.int32, (16, mass.shape[1]), 0)
    return jnp.where(row == 0, hi, jnp.where(row == 1, mass - hi, 0.0))


def numerators(me, distance, lhs, scaled, dtype, lanes):
    height = lhs.shape[0]
    width = height - 16

    def kern(me_ref, l_ref, a_ref, o_ref):
        chunk = (coordinates(me_ref)[1] + distance) & 3
        for q in range(scaled.shape[1] // lanes):

            @pl.when(chunk == q)
            def _():
                at = slice(q * lanes, (q + 1) * lanes)
                out = lax.dot_general(l_ref[...], a_ref[:, at], NN, preferred_element_type=F32)
                mass = jnp.sum(out[width:], axis=0, keepdims=True)
                o_ref[pl.ds(0, width), :] = out[:width].astype(dtype)
                o_ref[pl.ds(width, 16), :] = mass_rows(mass).astype(dtype)

    return pl.pallas_call(
        kern,
        out_shape=jax.ShapeDtypeStruct((height, lanes), dtype),
        in_specs=[SCALARS, WHOLE, WHOLE],
        out_specs=WHOLE,
        compiler_params=params(12),
        cost_estimate=cost(1000),
        name="numerators",
    )(me, held(lhs), held(scaled))


def add_first(me, own, arrived):
    height, lanes = own.shape
    width = height - 16
    piece = lanes // 4

    def kern(me_ref, own_ref, r1, r2, r3, *outs):
        for d in range(4):
            at = pl.ds(pl.multiple_of(((coordinates(me_ref)[2] + d) & 3) * piece, piece), piece)
            total = own_ref[:, at]
            for r in (r1, r2, r3):
                total = total + r[:, at].astype(F32)
            mass = jnp.sum(total[width:], axis=0, keepdims=True)
            outs[d][pl.ds(0, width), :] = total[:width].astype(outs[d].dtype)
            outs[d][pl.ds(width, 16), :] = mass_rows(mass).astype(outs[d].dtype)

    return pl.pallas_call(
        kern,
        out_shape=[jax.ShapeDtypeStruct((height, piece), F32 if d == 0 else BF) for d in range(4)],
        in_specs=[SCALARS] + [WHOLE] * 4,
        out_specs=[WHOLE] * 4,
        compiler_params=params(12),
        name="add_first",
    )(me, own, *arrived)


def add_second(own, arrived):
    height, lanes = own.shape
    width = height - 16

    def kern(own_ref, r1, r2, r3, o_ref):
        total = own_ref[...]
        for r in (r1, r2, r3):
            total = total + r[...].astype(F32)
        mass = jnp.sum(total[width:], axis=0, keepdims=True)
        o_ref[...] = (total[:width] / mass).T.astype(BF)

    return pl.pallas_call(
        kern,
        out_shape=jax.ShapeDtypeStruct((lanes, width), BF),
        in_specs=[WHOLE] * 4,
        out_specs=WHOLE,
        compiler_params=params(12),
        name="add_second",
    )(own, *arrived)


def pair(upper, lower):
    rows, width = upper.shape

    def kern(u_ref, l_ref, o_ref):
        o_ref[:rows, :] = u_ref[...]
        o_ref[rows:, :] = l_ref[...]

    return pl.pallas_call(
        kern,
        out_shape=jax.ShapeDtypeStruct((2 * rows, width), upper.dtype),
        in_specs=[WHOLE] * 2,
        out_specs=WHOLE,
        compiler_params=params(8),
        name="pair",
    )(upper, lower)


def assemble(base, shape, pairs, me):
    count = len(pairs)
    rows = pairs[0][0].shape[0] // 2

    def kern(me_ref, *refs):
        core, first, second = coordinates(me_ref)
        o_ref, sems = refs[-2], refs[-1]
        copies = []
        for i, (_, other, back, halves) in enumerate(pairs):
            a, b, c = (1 - core, second, first) if other else (core, first, second)
            for h in range(2):
                index = a * 16 + ((b - back) & 3) * 4 + ((c - halves[h]) & 3)
                at = pl.ds(pl.multiple_of(index * rows, rows), rows)
                copies.append(
                    pltpu.make_async_copy(refs[i].at[pl.ds(h * rows, rows), :], o_ref.at[at, :], sems.at[2 * i + h])
                )
        for c in copies:
            c.start()
        for c in copies:
            c.wait()

    given = [] if base is None else [base]
    return pl.pallas_call(
        kern,
        out_shape=jax.ShapeDtypeStruct(shape, pairs[0][0].dtype),
        in_specs=[SCALARS] + [WHOLE] * count + [ANYWHERE] * len(given),
        out_specs=ANYWHERE,
        scratch_shapes=[pltpu.SemaphoreType.DMA((2 * count,))],
        input_output_aliases={} if base is None else {1 + count: 0},
        compiler_params=params(8),
        name="assemble",
    )(me, *[held(p) for p, _, _, _ in pairs], *given)


def per_device(features, codebook):
    me = lax.axis_index("pts").astype(jnp.int32).reshape(1)
    codes = codebook.shape[0] // 2
    total_rows = features.shape[0] * lax.axis_size("pts")
    total_codes = codebook.shape[0] * lax.axis_size("code")
    target = math.log(total_rows / total_codes)

    theirs = other_core(features)
    lse_own, half = columns_first(me, features, codebook, codes)
    lse, feats_t = columns(features, theirs, half, lse_own)

    def over_chips(value):
        group = [[place(a, b, c) for a in range(4) for b in range(4)] for c in range(2)]
        return lax.all_to_all(value, "pts", 0, 0, tiled=True, axis_index_groups=group)

    def across(value):
        group = [
            [place(a, b, c) * 4 + z for c in range(2) for z in range(4)]
            for a in range(4) for b in range(4)
        ]
        return lax.all_to_all(value, ("pts", "code"), 0, 0, tiled=True, axis_index_groups=group)

    scale = math.exp(target)
    scaled, lses, peak, first_col = rows_first(me, features, theirs, half, over_chips(lse), target)
    sums, first_row, weight = col_sums_first(me, scaled, across(lses), peak)
    totals, _ = row_sums(me, scaled, weight, over_chips(sums), first_col, scale)
    sums = col_sums(me, scaled, across(totals), weight)
    totals, col_pot = row_sums(me, scaled, weight, over_chips(sums), first_col, scale)
    totals, col_pot, feats_t = lax.optimization_barrier((across(totals), col_pot, feats_t))
    lhs, row_pot = weigh(me, feats_t, totals, weight, first_row)

    arrived = []
    for d in (3, 1, 2):
        arrived.append(first_axis(numerators(me, d, lhs, scaled, BF, codes // 4), d))
    own = numerators(me, 0, lhs, scaled, F32, codes // 4)
    pieces = add_first(me, own, arrived)
    arrived = [second_axis(pieces[d], d) for d in (2, 1, 3)]
    fresh = add_second(pieces[0], arrived)

    my_rows = row_pot.reshape(-1)
    their_col = other_core(col_pot)
    cols = jnp.where(me[0] & 1 == 0, jnp.stack([col_pot, their_col]), jnp.stack([their_col, col_pot])).reshape(-1)
    fresh, my_rows, cols = lax.optimization_barrier((fresh, my_rows, cols))

    one, three, two = lax.optimization_barrier(tuple(second_axis(fresh, d) for d in (1, 3, 2)))
    near, far = pair(fresh, one), pair(three, two)

    def placed(value, back, kind):
        halves = (0, 1) if kind == 0 else (3, 2)
        return [
            (value, False, back, halves),
            (other_core(value), True, back, halves),
        ]

    near_1, far_3 = first_axis(near, 1), first_axis(far, 3)
    far_1, near_3 = first_axis(far, 1), first_axis(near, 3)
    near_2, far_2 = first_axis(near_1, 1), first_axis(far_3, 3)
    out = assemble(None, codebook.shape, placed(near, 0, 0) + placed(far, 0, 1), me)
    out = assemble(out, codebook.shape, placed(near_1, 1, 0) + placed(far_3, 3, 1), me)
    rest = placed(far_1, 1, 1) + placed(near_3, 3, 0) + placed(near_2, 2, 0) + placed(far_2, 2, 1)
    out = assemble(out, codebook.shape, rest, me)
    return out, my_rows, cols


def solution(mesh):
    return jax.shard_map(
        per_device,
        mesh=mesh,
        in_specs=(P("pts", None), P("code", None)),
        out_specs=(P("code", None), P("pts"), P("code")),
        check_vma=False,
    )
```
